32 devices in a mesh: section: 2 (over core), tensor: 4 (over y, x), dp: 4 (over z).
Axes of the slice: x: 2, y: 2, z: 4, core: 2. Of those that a mesh axis runs over, the one named last changes fastest.
Arguments:
- tokens: bfloat16 [2048, 640], P('dp'), may hold values from -6 to 6
- segments: int32 [2048], P('dp'), may hold values from 0 to 100255, as said below
- cotangent: bfloat16 [2048, 640], P('dp'), may hold values from -6 to 6
- w_query: bfloat16 [2, 640, 1024], P('section', None, 'tensor'), may hold values from -0.25 to 0.25
- w_key: bfloat16 [2, 640, 256], P('section'), may hold values from -0.25 to 0.25
- w_value: bfloat16 [2, 640, 256], P('section'), may hold values from -0.25 to 0.25
- w_out: bfloat16 [2, 1024, 640], P('section', 'tensor'), may hold values from -0.1875 to 0.1875
- w_gate: bfloat16 [2, 640, 2048], P('section', None, 'tensor'), may hold values from -0.25 to 0.25
- w_up: bfloat16 [2, 640, 2048], P('section', None, 'tensor'), may hold values from -0.25 to 0.25
- w_down: bfloat16 [2, 2048, 640], P('section', 'tensor'), may hold values from -0.125 to 0.125
- norm_gains: float32 [2, 4, 640], P('section'), may hold values from 0.25 to 1.75
- head_gains: float32 [2, 2, 256], P('section'), may hold values from 0.25 to 1.75
Outputs:
- section_out: float32 [2, 2048, 640], P('section', 'dp')
- input_grad: float32 [2, 2048, 640], P('section', 'dp')
- grad_query: float32 [2, 640, 1024], P('section', 'dp', 'tensor')
- grad_key: float32 [2, 640, 256], P('section')
- grad_value: float32 [2, 640, 256], P('section')
- grad_out: float32 [2, 1024, 640], P('section', 'tensor', 'dp')
- grad_gate: float32 [2, 640, 2048], P('section', 'dp', 'tensor')
- grad_up: float32 [2, 640, 2048], P('section', 'dp', 'tensor')
- grad_down: float32 [2, 2048, 640], P('section', 'tensor', 'dp')
- grad_norm_gains: float32 [2, 4, 640], P('section', None, 'dp')
- grad_head_gains: float32 [2, 2, 256], P('section')
The draws below stay inside these ranges and needn't reach their ends.
Inputs may be any that keep to these rules, and one draw needn't show every extreme that they name: `segments`: split tokens into rows of 256 in order (one micro-batch of one data rank each). In every row the real tokens come first: their ids start at 0 at the row's first token and rise by one at each new sequence, so that each sequence is contiguous; the rest of the row is padding, at least one token, each with its own id 100000 plus its place in the row.
All inputs are finite; a program needn't handle non-finite values.
Results may differ from the reference program's by a relative error of at most 0.025.
Values may be sent and summed in bfloat16 or wider, within the bound.
A program may use at most 128 MiB of HBM per device.

```python
import math
import jax
import jax.numpy as jnp
from jax import lax

D = 640
HEADS = 4
HD = 256
FF = 2048
WINDOW = 512
MB_TOK = 256
MICRO = 2
TOKENS = 2048
N_TENSOR = 4
N_DP = 4


def draw_segments(key, part):
    key = jax.random.fold_in(key, 11)
    row_count = N_DP * MICRO
    pad_key, cut_key, long_key, pick_key, span_key, place_key = jax.random.split(key, 6)
    padding = jax.random.randint(pad_key, (row_count, 1), 1, MB_TOK // 16 + 2).astype(jnp.int32)
    real_len = MB_TOK - padding
    least_len = jnp.minimum(real_len, WINDOW + WINDOW // 8)
    span = jax.random.randint(span_key, (row_count, 1), least_len, real_len + 1).astype(jnp.int32)
    offset = jax.random.randint(place_key, (row_count, 1), 0, real_len - span + 1).astype(jnp.int32)
    chosen = jax.random.randint(pick_key, (), 0, row_count).astype(jnp.int32)
    row_numbers = jnp.arange(row_count, dtype=jnp.int32)[:, None]
    long_row = (jax.random.randint(long_key, (row_count, 1), 0, 2) == 0) | (row_numbers == chosen)
    indices = jnp.arange(MB_TOK, dtype=jnp.int32)[None, :]
    starts = (jax.random.randint(cut_key, (row_count, MB_TOK), 0, MB_TOK // 3) == 0).astype(jnp.int32)
    inside = long_row & (indices > offset) & (indices < offset + span)
    edges = long_row & ((indices == offset) | (indices == offset + span))
    starts = jnp.where(inside, 0, jnp.where(edges, 1, starts))
    starts = jnp.where(indices == 0, 0, starts)
    numbers = jnp.cumsum(starts, axis=1).astype(jnp.int32)
    labels = jnp.where(indices < real_len, numbers, 100000 + indices)
    return labels.reshape(row_count * MB_TOK).astype(jnp.int32)


def levels(rng, extent, cuts, smallest, high):
    def one(axis_at, parts):
        heights = jax.random.uniform(jax.random.fold_in(jax.random.fold_in(rng, 6), axis_at), (parts,), jnp.float32, smallest / len(cuts), high / len(cuts))
        return jnp.repeat(jnp.exp(heights), extent[axis_at] // parts).reshape((-1,) + (1,) * (len(extent) - axis_at - 1))

    gain = one(*cuts[0])
    for cut in cuts[1:]:
        gain = gain * one(*cut)
    return gain


def scatter_about(key, dims, spread, bound, cuts=(), kind=jnp.bfloat16):
    array = spread * jax.random.normal(key, dims, jnp.float32)
    if cuts:
        array = array * levels(key, dims, cuts, -0.22, 0.18)
    return jnp.clip(array, -bound, bound).astype(kind)


def setup_inputs(seed: int = 0) -> dict:
    key_list = jax.random.split(jax.random.key(seed), 13)
    tokens = scatter_about(key_list[0], (TOKENS, D), 1.0, 6.0, ((0, 4),))
    segments = draw_segments(jax.random.fold_in(key_list[12], 71), 0)
    cotangent = scatter_about(key_list[2], (TOKENS, D), 1.0, 6.0, ((0, 4),))
    w_query = scatter_about(key_list[3], (2, D, HEADS * HD), D ** -0.5, 0.25, ((0, 2), (2, 4)))
    w_key = scatter_about(key_list[4], (2, D, HD), D ** -0.5, 0.25, ((0, 2),))
    w_value = scatter_about(key_list[5], (2, D, HD), D ** -0.5, 0.25, ((0, 2),))
    w_out = scatter_about(key_list[6], (2, HEADS * HD, D), (HEADS * HD) ** -0.5, 0.1875, ((0, 2), (1, 4)))
    w_gate = scatter_about(key_list[7], (2, D, FF), D ** -0.5, 0.25, ((0, 2), (2, 4)))
    w_up = scatter_about(key_list[8], (2, D, FF), D ** -0.5, 0.25, ((0, 2), (2, 4)))
    w_down = scatter_about(key_list[9], (2, FF, D), FF ** -0.5, 0.125, ((0, 2), (1, 4)))
    norm_gains = jnp.clip(1.0 + 0.15 * jax.random.normal(key_list[10], (2, 4, D), jnp.float32), 0.25, 1.75)
    head_gains = jnp.clip(1.0 + 0.15 * jax.random.normal(key_list[11], (2, 2, HD), jnp.float32), 0.25, 1.75)
    return {"tokens": tokens, "segments": segments, "cotangent": cotangent, "w_query": w_query, "w_key": w_key, "w_value": w_value, "w_out": w_out, "w_gate": w_gate, "w_up": w_up, "w_down": w_down, "norm_gains": norm_gains, "head_gains": head_gains}


@jax.custom_vjp
def low(v):
    return lax.optimization_barrier(v.astype(jnp.bfloat16)).astype(jnp.float32)

@jax.custom_vjp
def low_back(v):
    return v

def low_keep(v):
    return (low(v), None)

def low_pass(kept, grad):
    return (grad,)

def back_keep(v):
    return (v, None)

def back_low(kept, grad):
    return (low(grad),)
low.defvjp(low_keep, low_pass)
low_back.defvjp(back_keep, back_low)
EPSILON = 1e-06
PRECISE = lax.Precision.HIGHEST

def norm_rows(values):
    return values * lax.rsqrt(lax.optimization_barrier(jnp.mean(values * values, axis=-1, keepdims=True)) + EPSILON)

def frequencies(head_width):
    half_width = head_width // 2
    return jnp.exp(jnp.arange(half_width, dtype=jnp.float32) * (-2.0 * math.log(10000.0) / head_width))

def rotary(values, angles):
    half_width = values.shape[-1] // 2
    front_half = values[..., :half_width]
    back_half = values[..., half_width:]
    cosine = jnp.cos(angles)
    sine_part = jnp.sin(angles)
    return jnp.concatenate([front_half * cosine - back_half * sine_part, back_half * cosine + front_half * sine_part], axis=-1)

def row_layout(doc_ids):
    indices = jnp.arange(doc_ids.shape[0], dtype=jnp.int32)
    same_doc = doc_ids[:, None] == doc_ids[None, :]
    before = indices[None, :] <= indices[:, None]
    positions = lax.optimization_barrier(jnp.sum((same_doc & before).astype(jnp.int32), axis=1)) - 1
    allowed = same_doc & before & (indices[:, None] - indices[None, :] < WINDOW)
    return (allowed, positions)

def layer_row(layer_in, doc_ids, weights):
    w_query, w_key, w_value, w_out, w_gate, w_up, w_down, norm_gains, head_gains = weights
    row_count = layer_in.shape[0]
    allowed, positions = row_layout(doc_ids)
    angles = positions.astype(jnp.float32)[:, None] * frequencies(HD)[None, :]
    group_heads = HEADS // N_TENSOR
    group_units = FF // N_TENSOR
    score_scale = HD ** (-0.5)
    normed = low(norm_rows(layer_in) * norm_gains[0])
    attended = jnp.zeros_like(layer_in)
    for member in range(N_TENSOR):
        columns = slice(member * group_heads * HD, (member + 1) * group_heads * HD)
        queries = low_back(jnp.dot(normed, w_query[:, columns], precision=PRECISE)).reshape(row_count, group_heads, HD)
        key_rows = low_back(jnp.dot(normed, w_key, precision=PRECISE))
        values = low(low_back(jnp.dot(normed, w_value, precision=PRECISE)))
        queries = low(rotary(norm_rows(queries) * head_gains[0], angles[:, None, :]))
        key_rows = low(rotary(norm_rows(key_rows) * head_gains[1], angles))
        scores = low_back(jnp.einsum('qhd,kd->hqk', queries, key_rows, precision=PRECISE) * score_scale)
        attn_prob = low(jax.nn.softmax(jnp.where(allowed[None], scores, -1e+30), axis=-1))
        mixed_heads = low(low_back(jnp.einsum('hqk,kd->qhd', attn_prob, values, precision=PRECISE)))
        attn_part = jnp.dot(mixed_heads.reshape(row_count, group_heads * HD), w_out[columns, :], precision=PRECISE)
        attended = attended + low_back(attn_part)
    residual = layer_in + norm_rows(attended) * norm_gains[1]
    normed_mlp = low(norm_rows(residual) * norm_gains[2])
    mlp_sum = jnp.zeros_like(layer_in)
    for member in range(N_TENSOR):
        columns = slice(member * group_units, (member + 1) * group_units)
        gate_raw = low_back(jnp.dot(normed_mlp, w_gate[:, columns], precision=PRECISE))
        up_raw = low_back(jnp.dot(normed_mlp, w_up[:, columns], precision=PRECISE))
        hidden = low(jax.nn.gelu(gate_raw, approximate=True) * up_raw)
        mlp_part = jnp.dot(hidden, w_down[columns, :], precision=PRECISE)
        mlp_sum = mlp_sum + low_back(mlp_part)
    return residual + norm_rows(mlp_sum) * norm_gains[3]

def layer(layer_in, doc_ids, weights):

    def one_row(paired):
        return layer_row(paired[0], paired[1], weights)
    return lax.map(jax.checkpoint(one_row), (layer_in, doc_ids))

def reference(tokens, segments, cotangent, w_query, w_key, w_value, w_out, w_gate, w_up, w_down, norm_gains, head_gains):
    row_count = N_DP * MICRO
    first_in = tokens.astype(jnp.float32).reshape(row_count, MB_TOK, D)
    doc_ids = segments.reshape(row_count, MB_TOK)
    last_grad = cotangent.astype(jnp.float32).reshape(row_count, MB_TOK, D)
    arrays = (w_query, w_key, w_value, w_out, w_gate, w_up, w_down, norm_gains, head_gains)

    def weights_of(section_idx):
        return tuple((item[section_idx].astype(jnp.float32) for item in arrays))

    def run_layer(layer_in, weights):
        return layer(layer_in, doc_ids, weights)
    first_out, first_back = jax.vjp(run_layer, first_in, weights_of(0))
    middle_in = low(first_out)
    second_out, second_back = jax.vjp(run_layer, middle_in, weights_of(1))
    middle_full, second_grads = second_back(last_grad)
    middle_grad = low(middle_full)
    first_grad, first_grads = first_back(middle_grad)
    section_out = jnp.stack([first_out, second_out]).reshape(2, TOKENS, D).astype(jnp.float32)
    input_grad = jnp.stack([first_grad, middle_full]).reshape(2, TOKENS, D).astype(jnp.float32)
    stacked = [jnp.stack([first_grads[number], second_grads[number]]).astype(jnp.float32) for number in range(9)]
    return (section_out, input_grad, stacked[0], stacked[1], stacked[2], stacked[3], stacked[4], stacked[5], stacked[6], stacked[7], stacked[8])
```

```python
import functools
import math

import jax
import jax.numpy as jnp
from jax import lax
from jax.experimental import pallas as pl
from jax.experimental.pallas import tpu as pltpu
from jax.sharding import PartitionSpec as P

WINDOW = 512
MB_TOK = 256
EPSILON = 1e-06
BF = jnp.bfloat16
F32 = jnp.float32
MESH = pl.DeviceIdType.MESH
VM = pl.BlockSpec(memory_space=pltpu.VMEM)
ANY = pl.BlockSpec(memory_space=pl.ANY)
VMEM_LIMIT = 50 * 1024 * 1024


def mm(a, b):
    return lax.dot_general(a, b, (((1,), (0,)), ((), ())), preferred_element_type=F32)


def mm_t(a, b):
    return lax.dot_general(a, b, (((1,), (1,)), ((), ())), preferred_element_type=F32)


def t_mm(a, b):
    return lax.dot_general(a, b, (((0,), (0,)), ((), ())), preferred_element_type=F32)


def inverse_rms(v):
    return lax.rsqrt(jnp.mean(v * v, axis=-1, keepdims=True) + EPSILON)


def rms(v):
    return v * inverse_rms(v)


def rms_back(v, gain, cot):
    inv = inverse_rms(v)
    unit = v * inv
    weighted = cot * gain
    d_v = inv * (weighted - unit * jnp.mean(weighted * unit, axis=-1, keepdims=True))
    return d_v, jnp.sum(cot * unit, axis=0, keepdims=True)


def rope(u, cos, sin):
    half = u.shape[-1] // 2
    a, b = u[:, :half], u[:, half:]
    return jnp.concatenate([a * cos - b * sin, b * cos + a * sin], axis=-1)


def rope_back(d, cos, sin):
    half = d.shape[-1] // 2
    a, b = d[:, :half], d[:, half:]
    return jnp.concatenate([a * cos + b * sin, b * cos - a * sin], axis=-1)


GELU_C = math.sqrt(2.0 / math.pi)


def gelu_parts(g):
    th = jnp.tanh(GELU_C * (g + 0.044715 * g * g * g))
    value = 0.5 * g * (1.0 + th)
    slope = 0.5 * (1.0 + th) + 0.5 * g * (1.0 - th * th) * GELU_C * (1.0 + 3 * 0.044715 * g * g)
    return value, slope


def call_exchange(ins, out_shapes, gathered, pre, during, shard, ranks, collective_id):
    n_in, n_out = len(ins), len(out_shapes)
    rows, width = MB_TOK, ins[0].shape[-1]
    share = rows // ranks

    def kernel(*refs):
        in_refs = refs[:n_in]
        gat = refs[n_in : n_in + gathered]
        outs = refs[n_in + gathered : n_in + gathered + n_out]
        part, recv, rs_send, rs_recv, ag_send, ag_recv = refs[n_in + gathered + n_out :]
        me = lax.axis_index("tensor")
        peers = [lax.rem(me + d, ranks) for d in range(1, ranks)]
        barrier = pltpu.get_barrier_semaphore()
        for peer in peers:
            pl.semaphore_signal(barrier, inc=1, device_id={"tensor": peer}, device_id_type=MESH)
        own = pl.ds(pl.multiple_of(me * share, share), share)
        part[...] = pre(in_refs, outs).astype(BF)
        pl.semaphore_wait(barrier, ranks - 1)
        copies = []
        for d, peer in enumerate(peers):
            copy = pltpu.make_async_remote_copy(
                src_ref=part.at[pl.ds(pl.multiple_of(peer * share, share), share)],
                dst_ref=recv.at[d],
                send_sem=rs_send.at[d],
                recv_sem=rs_recv.at[d],
                device_id={"tensor": peer},
                device_id_type=MESH,
            )
            copy.start()
            copies.append(copy)
        if during is not None:
            during(in_refs, outs)
        total = part[own].astype(F32)
        for d, copy in enumerate(copies):
            copy.wait_recv()
            total = total + recv[d].astype(F32)
        results = shard(total, own, in_refs, outs)
        sends = []
        for i in range(gathered):
            gat[i][own] = results[i]
            for d, peer in enumerate(peers):
                copy = pltpu.make_async_remote_copy(
                    src_ref=gat[i].at[own],
                    dst_ref=gat[i].at[own],
                    send_sem=ag_send.at[i, d],
                    recv_sem=ag_recv.at[i, d],
                    device_id={"tensor": peer},
                    device_id_type=MESH,
                )
                copy.start()
                sends.append(copy)
        for copy in copies:
            copy.wait_send()
        for copy in sends:
            copy.wait()

    return pl.pallas_call(
        kernel,
        out_shape=[jax.ShapeDtypeStruct((rows, width), BF)] * gathered + out_shapes,
        in_specs=[VM] * n_in,
        out_specs=[VM] * (gathered + n_out),
        scratch_shapes=[
            pltpu.VMEM((rows, width), BF),
            pltpu.VMEM((ranks - 1, share, width), BF),
            pltpu.SemaphoreType.DMA((ranks - 1,)),
            pltpu.SemaphoreType.DMA((ranks - 1,)),
            pltpu.SemaphoreType.DMA((gathered, ranks - 1)),
            pltpu.SemaphoreType.DMA((gathered, ranks - 1)),
        ],
        compiler_params=pltpu.CompilerParams(
            collective_id=collective_id, has_side_effects=True, vmem_limit_bytes=VMEM_LIMIT
        ),
    )(*ins)


def swap_kernel(count, *refs):
    ins, firsts, seconds = refs[:count], refs[count : 2 * count], refs[2 * count : 3 * count]
    local_sem, send_sem, recv_sem = refs[3 * count :]
    me = lax.axis_index("section")
    other = 1 - me
    barrier = pltpu.get_barrier_semaphore()
    pl.semaphore_signal(barrier, inc=1, device_id={"section": other}, device_id_type=MESH)
    pl.semaphore_wait(barrier, 1)
    for sec, outs in ((0, firsts), (1, seconds)):

        @pl.when(me == sec)
        def _():
            copies = []
            for i in range(count):
                far = pltpu.make_async_remote_copy(
                    src_ref=ins[i],
                    dst_ref=outs[i],
                    send_sem=send_sem.at[i],
                    recv_sem=recv_sem.at[i],
                    device_id={"section": other},
                    device_id_type=MESH,
                )
                near = pltpu.make_async_copy(ins[i], outs[i], local_sem.at[i])
                far.start()
                near.start()
                copies += [far, near]
            for copy in copies:
                copy.wait()


def both_layers(weights):
    count = len(weights)
    shapes = [jax.ShapeDtypeStruct(w.shape, w.dtype) for w in weights]
    outs = pl.pallas_call(
        functools.partial(swap_kernel, count),
        out_shape=shapes * 2,
        in_specs=[ANY] * count,
        out_specs=[ANY] * (2 * count),
        scratch_shapes=[pltpu.SemaphoreType.DMA((count,))] * 3,
        compiler_params=pltpu.CompilerParams(collective_id=1, has_side_effects=True),
    )(*weights)
    return outs[:count], outs[count:]


def struct(shape, dtype=F32):
    return jax.ShapeDtypeStruct(shape, dtype)


def attend_forward(x16, w, tables, ranks, cid):
    w_query, w_key, w_value, w_out, _, _, _, norm_gains, head_gains = w
    cos, sin, seg_col, seg_row = tables
    width = x16.shape[1]
    hd = w_key.shape[-1]
    rows = MB_TOK

    def pre(i, o):
        x_ref, wq, wk, wv, wo, ng, hg, cos, sin, sc, sr = i
        n1_o, qr_o, kr_o, q_o, k_o, v_o, p_o, mix_o = o[:8]
        n1 = (rms(x_ref[...].astype(F32)) * ng[0, 0:1]).astype(BF)
        n1_o[...] = n1
        qr = mm(n1, wq[0])
        kr = mm(n1, wk[0])
        v = mm(n1, wv[0]).astype(BF)
        qr_o[...] = qr
        kr_o[...] = kr
        v_o[...] = v
        q = rope(rms(qr) * hg[0, 0:1], cos[...], sin[...]).astype(BF)
        k = rope(rms(kr) * hg[0, 1:2], cos[...], sin[...]).astype(BF)
        q_o[...] = q
        k_o[...] = k
        at = lax.broadcasted_iota(jnp.int32, (rows, rows), 0)
        to = lax.broadcasted_iota(jnp.int32, (rows, rows), 1)
        allowed = (sc[...] == sr[...]) & (to <= at) & (at - to < WINDOW)
        s = jnp.where(allowed, mm_t(q, k) * (hd**-0.5), -1e30)
        e = jnp.exp(s - jnp.max(s, axis=-1, keepdims=True))
        p = e / jnp.sum(e, axis=-1, keepdims=True)
        p_o[...] = p
        mix = mm(p.astype(BF), v).astype(BF)
        mix_o[...] = mix
        return mm(mix, wo[0])

    def shard(total, own, i, o):
        ng = i[5]
        residual = i[0][own].astype(F32) + rms(total) * ng[0, 1:2]
        o[8][...] = total
        o[9][...] = residual
        return [(rms(residual) * ng[0, 2:3]).astype(BF)]

    share = rows // ranks
    return call_exchange(
        [x16, w_query, w_key, w_value, w_out, norm_gains, head_gains, cos, sin, seg_col, seg_row],
        [
            struct((rows, width), BF),
            struct((rows, hd)),
            struct((rows, hd)),
            struct((rows, hd), BF),
            struct((rows, hd), BF),
            struct((rows, hd), BF),
            struct((rows, rows)),
            struct((rows, hd), BF),
            struct((share, width)),
            struct((share, width)),
        ],
        1, pre, None, shard, ranks, cid,
    )


def feed_forward(n2, residual, w, cot, ranks, cid):
    _, _, _, _, w_gate, w_up, w_down, norm_gains, _ = w
    width = n2.shape[1]
    units = w_gate.shape[-1]
    rows = MB_TOK
    share = rows // ranks

    def pre(i, o):
        n2_ref, res, wg, wu, wd, ng = i[:6]
        n2 = n2_ref[...]
        gate = mm(n2, wg[0])
        up = mm(n2, wu[0])
        h = (gelu_parts(gate)[0] * up).astype(BF)
        o[0][...] = gate
        o[1][...] = up
        o[2][...] = h
        return mm(h, wd[0])

    def shard(total, own, i, o):
        res, ng = i[1], i[5]
        gain = ng[0, 3:4]
        y16 = (res[...] + rms(total) * gain).astype(BF)
        o[3][...] = total
        if cot is None:
            return [y16]
        d_mlp, d_gain = rms_back(total, gain, i[6][own].astype(F32))
        o[4][...] = d_gain
        return [y16, d_mlp.astype(BF)]

    outs = [struct((rows, units)), struct((rows, units)), struct((rows, units), BF), struct((share, width))]
    ins = [n2, residual, w_gate, w_up, w_down, norm_gains]
    if cot is not None:
        ins.append(cot)
        outs.append(struct((1, width)))
    return call_exchange(ins, outs, 1 if cot is None else 2, pre, None, shard, ranks, cid)


def feed_backward(d_mlp16, dy16, kept, w, ranks, cid):
    _, _, _, _, w_gate, w_up, w_down, norm_gains, _ = w
    n2, gate, up, h, residual, attended = kept
    width = n2.shape[1]
    units = w_gate.shape[-1]
    rows = MB_TOK
    share = rows // ranks

    def pre(i, o):
        dm, _, _, gate, up, _, _, _, wg, wu, wd, _ = i
        dh = mm_t(dm[...], wd[0])
        value, slope = gelu_parts(gate[...])
        dg = (dh * up[...] * slope).astype(BF)
        du = (dh * value).astype(BF)
        o[4][...] = dg
        o[5][...] = du
        return mm_t(dg, wg[0]) + mm_t(du, wu[0])

    def during(i, o):
        dm, n2, h = i[0], i[2], i[5]
        o[0][:, :units] = t_mm(n2[...], o[4][...]).astype(BF)
        o[0][:, units : 2 * units] = t_mm(n2[...], o[5][...]).astype(BF)
        o[0][:, 2 * units :] = t_mm(dm[...], h[...]).astype(BF)

    def shard(total, own, i, o):
        dy, res, att, ng = i[1], i[6], i[7], i[11]
        d_branch, dg2 = rms_back(res[...], ng[0, 2:3], total)
        dr = dy[own].astype(F32) + d_branch
        d_att, dg1 = rms_back(att[...], ng[0, 1:2], dr)
        o[1][...] = dr
        o[2][...] = dg1
        o[3][...] = dg2
        return [d_att.astype(BF)]

    return call_exchange(
        [d_mlp16, dy16, n2, gate, up, h, residual, attended, w_gate, w_up, w_down, norm_gains],
        [
            struct((width, 3 * units), BF),
            struct((share, width)),
            struct((1, width)),
            struct((1, width)),
            struct((rows, units), BF),
            struct((rows, units), BF),
        ],
        1, pre, during, shard, ranks, cid,
    )


def attend_backward(d_att16, dr, x16, kept, w, tables, below, ranks, cid):
    w_query, w_key, w_value, w_out, _, _, _, norm_gains, head_gains = w
    n1, qr, kr, q, k, v, p, mix = kept
    cos, sin = tables[:2]
    width = n1.shape[1]
    hd = w_key.shape[-1]
    rows = MB_TOK

    def pre(i, o):
        da, _, _, n1, qr, kr, q, k, v, p, mix, cos, sin, wq, wk, wv, wo, _, hg = i[:19]
        scale = hd**-0.5
        do = mm_t(da[...], wo[0]).astype(BF)
        p = p[...]
        d_p = mm_t(do, v[...])
        ds = (p * (d_p - jnp.sum(p * d_p, axis=-1, keepdims=True))).astype(BF)
        dq = mm(ds, k[...]) * scale
        dk = t_mm(ds, q[...]) * scale
        dv = t_mm(p.astype(BF), do).astype(BF)
        dq_raw, dgq = rms_back(qr[...], hg[0, 0:1], rope_back(dq, cos[...], sin[...]))
        dk_raw, dgk = rms_back(kr[...], hg[0, 1:2], rope_back(dk, cos[...], sin[...]))
        dq_raw = dq_raw.astype(BF)
        dk_raw = dk_raw.astype(BF)
        o[2][...] = dgq
        o[3][...] = dgk
        o[4][...] = dq_raw
        o[5][...] = dk_raw
        o[6][...] = dv
        return mm_t(dq_raw, wq[0]) + mm_t(dk_raw, wk[0]) + mm_t(dv, wv[0])

    def during(i, o):
        da, n1, mix = i[0][...], i[3][...], i[10][...]
        o[0][:, :hd] = t_mm(n1, o[4][...]).astype(BF)
        o[0][:, hd : 2 * hd] = t_mm(da, mix).astype(BF)
        o[0][:, 2 * hd : 3 * hd] = t_mm(n1, o[5][...]).astype(BF)
        o[0][:, 3 * hd :] = t_mm(n1, o[6][...]).astype(BF)

    def shard(total, own, i, o):
        d_branch, dg0 = rms_back(i[2][own].astype(F32), i[17][0, 0:1], total)
        o[1][...] = dg0
        dx16 = (i[1][...] + d_branch).astype(BF)
        if below is None:
            return [dx16]
        d_mlp, dg3 = rms_back(i[19][...], i[20][0, 3:4], dx16.astype(F32))
        o[7][...] = dg3
        return [dx16, d_mlp.astype(BF)]

    ins = [d_att16, dr, x16, n1, qr, kr, q, k, v, p, mix, cos, sin]
    ins += [w_query, w_key, w_value, w_out, norm_gains, head_gains]
    outs = [
        struct((width, 4 * hd), BF),
        struct((1, width)),
        struct((1, hd)),
        struct((1, hd)),
        struct((rows, hd), BF),
        struct((rows, hd), BF),
        struct((rows, hd), BF),
    ]
    if below is not None:
        ins += list(below)
        outs.append(struct((1, width)))
    return call_exchange(ins, outs, 1 if below is None else 2, pre, during, shard, ranks, cid)


def reduce_kernel(nt, nd, hd, *refs):
    (ga0, ga1, gm0, gm1, s0, s1, y0, y1, x0, x1) = refs[:10]
    (out_a, out_m, out_kv, out_s, out_y, out_x) = refs[10:16]
    (swap_a, swap_m, swap_s, h_a, h_m, r_a, r_m, kv_part, kv_recv, s_sum, s_recv) = refs[16:27]
    (sw_send, sw_recv, sm_send, sm_recv, lo_sem, dp_send, dp_recv, kt_send, kt_recv) = refs[27:36]
    (ka_send, ka_recv, ss_send, ss_recv) = refs[36:]
    sec = lax.axis_index("section")
    t = lax.axis_index("tensor")
    z = lax.axis_index("dp")
    total = nt * nd
    me = z * nt + t
    rows = ga0.shape[0] // nd
    section = {"section": 1 - sec}
    group = []
    for step in range(1, total):
        flat = lax.rem(me + step, total)
        group.append({"dp": flat // nt, "tensor": lax.rem(flat, nt)})
    barrier = pltpu.get_barrier_semaphore()
    for device in [section] + group:
        pl.semaphore_signal(barrier, inc=1, device_id=device, device_id_type=MESH)
    pl.semaphore_wait(barrier, total)

    def remote(src, dst, send, recv, device):
        return pltpu.make_async_remote_copy(
            src_ref=src, dst_ref=dst, send_sem=send, recv_sem=recv,
            device_id=device, device_id_type=MESH,
        )

    zs = [lax.rem(z + d, nd) for d in range(1, nd)] + [z]
    spans = [pl.ds(pl.multiple_of(peer * rows, rows), rows) for peer in zs]

    def swap(ga, gm, s, y, x):
        first = [remote(s, swap_s, sm_send.at[0], sm_recv.at[0], section)]
        for n, span in enumerate(spans):
            first.append(remote(ga.at[span], swap_a.at[span], sw_send.at[0, n], sw_recv.at[0, n], section))
        for n, span in enumerate(spans):
            first.append(remote(gm.at[span], swap_m.at[span], sw_send.at[1, n], sw_recv.at[1, n], section))
        first.append(remote(y, out_y.at[sec], sm_send.at[1], sm_recv.at[1], section))
        first.append(remote(x, out_x.at[sec], sm_send.at[2], sm_recv.at[2], section))
        return first

    @pl.when(sec == 0)
    def _():
        for copy in swap(ga1, gm1, s1, y1, x1):
            copy.start()
        pltpu.make_async_copy(y0, out_y.at[0], lo_sem.at[0]).start()
        pltpu.make_async_copy(x0, out_x.at[0], lo_sem.at[1]).start()

    @pl.when(sec == 1)
    def _():
        for copy in swap(ga0, gm0, s0, y0, x0):
            copy.start()
        pltpu.make_async_copy(y1, out_y.at[1], lo_sem.at[0]).start()
        pltpu.make_async_copy(x1, out_x.at[1], lo_sem.at[1]).start()

    waits = swap(ga0, gm0, s0, y0, x0)
    waits[0].wait_recv()

    @pl.when(sec == 0)
    def _():
        s_sum[...] = s0[...] + swap_s[...]

    @pl.when(sec == 1)
    def _():
        s_sum[...] = s1[...] + swap_s[...]

    s_copies = []
    for step, device in enumerate(group):
        copy = remote(s_sum, s_recv.at[step], ss_send.at[step], ss_recv.at[step], device)
        copy.start()
        s_copies.append(copy)
    dp_copies = []
    for kind, (g_0, g_1, got, held, landed) in enumerate(
        ((ga0, ga1, swap_a, h_a, r_a), (gm0, gm1, swap_m, h_m, r_m))
    ):
        for n in range(nd):
            waits[1 + kind * nd + n].wait_recv()
            span = spans[n]

            @pl.when(sec == 0)
            def _():
                held[n] = (g_0[span].astype(F32) + got[span].astype(F32)).astype(BF)

            @pl.when(sec == 1)
            def _():
                held[n] = (g_1[span].astype(F32) + got[span].astype(F32)).astype(BF)

            if n < nd - 1:
                copy = remote(
                    held.at[n], landed.at[n], dp_send.at[kind, n], dp_recv.at[kind, n], {"dp": zs[n]}
                )
                copy.start()
                dp_copies.append(copy)
    for n in range(nd - 1):
        dp_copies[n].wait_recv()
    acc = h_a[nd - 1].astype(F32)
    for n in range(nd - 1):
        acc = acc + r_a[n].astype(F32)
    out_a[...] = acc[:, : 2 * hd]
    piece = 2 * hd // nt
    for n in range(nt):
        kv_part[n] = acc[:, 2 * hd + n * piece : 2 * hd + (n + 1) * piece].astype(BF)
    kt_copies = []
    for d in range(1, nt):
        peer = lax.rem(t + d, nt)
        copy = remote(
            kv_part.at[peer], kv_recv.at[d - 1], kt_send.at[d - 1], kt_recv.at[d - 1], {"tensor": peer}
        )
        copy.start()
        kt_copies.append(copy)
    mine = kv_part[t].astype(F32)
    for d, copy in enumerate(kt_copies):
        copy.wait_recv()
        mine = mine + kv_recv[d].astype(F32)
    out_kv[me] = mine.astype(BF)
    ka_copies = []
    for step, device in enumerate(group):
        copy = remote(out_kv.at[me], out_kv.at[me], ka_send.at[step], ka_recv.at[step], device)
        copy.start()
        ka_copies.append(copy)
    acc_s = s_sum[...]
    for step, copy in enumerate(s_copies):
        copy.wait_recv()
        acc_s = acc_s + s_recv[step]
    out_s[...] = acc_s
    for n in range(nd - 1):
        dp_copies[nd - 1 + n].wait_recv()
    acc_m = h_m[nd - 1].astype(F32)
    for n in range(nd - 1):
        acc_m = acc_m + r_m[n].astype(F32)
    out_m[...] = acc_m
    waits[-2].wait_recv()
    waits[-1].wait_recv()
    pltpu.make_async_copy(y0, out_y.at[sec], lo_sem.at[0]).wait()
    pltpu.make_async_copy(x0, out_x.at[sec], lo_sem.at[1]).wait()
    for copy in ka_copies:
        copy.wait()
    for copy in waits + s_copies + dp_copies + kt_copies:
        copy.wait_send()


def reduce_all(grads_a, grads_m, smalls, ys, xs, nt, nd, hd):
    width, wa = grads_a[0].shape
    wm = grads_m[0].shape[1]
    rows = width // nd
    total = nt * nd
    dma = pltpu.SemaphoreType.DMA
    ins = list(grads_a) + list(grads_m) + list(smalls) + list(ys) + list(xs)
    tok = ys[0].shape
    return pl.pallas_call(
        functools.partial(reduce_kernel, nt, nd, hd),
        out_shape=[
            struct((rows, 2 * hd)),
            struct((rows, wm)),
            struct((total, rows, 2 * hd // nt), BF),
            struct(smalls[0].shape),
            struct((2,) + tok, BF),
            struct((2,) + tok, BF),
        ],
        in_specs=[VM] * len(ins),
        out_specs=[VM] * 6,
        scratch_shapes=[
            pltpu.VMEM((width, wa), BF),
            pltpu.VMEM((width, wm), BF),
            pltpu.VMEM(smalls[0].shape, F32),
            pltpu.VMEM((nd, rows, wa), BF),
            pltpu.VMEM((nd, rows, wm), BF),
            pltpu.VMEM((nd - 1, rows, wa), BF),
            pltpu.VMEM((nd - 1, rows, wm), BF),
            pltpu.VMEM((nt, rows, 2 * hd // nt), BF),
            pltpu.VMEM((nt - 1, rows, 2 * hd // nt), BF),
            pltpu.VMEM(smalls[0].shape, F32),
            pltpu.VMEM((total - 1,) + smalls[0].shape, F32),
            dma((2, nd)), dma((2, nd)), dma((3,)), dma((3,)), dma((2,)),
            dma((2, nd - 1)), dma((2, nd - 1)), dma((nt - 1,)), dma((nt - 1,)),
            dma((total - 1,)), dma((total - 1,)), dma((total - 1,)), dma((total - 1,)),
        ],
        compiler_params=pltpu.CompilerParams(
            collective_id=2, has_side_effects=True, vmem_limit_bytes=VMEM_LIMIT
        ),
    )(*ins)


def reduce_plain(grads_a, grads_m, smalls, ys, xs, nt, nd, hd):
    sec = lax.axis_index("section")
    pairs = [(0, 1), (1, 0)]

    def own_sum(pair):
        own = jnp.where(sec == 0, pair[0], pair[1])
        other = jnp.where(sec == 0, pair[1], pair[0])
        return own.astype(F32) + lax.ppermute(other, "section", pairs).astype(F32)

    def placed(pair):
        own = jnp.where(sec == 0, pair[0], pair[1])
        other = lax.ppermute(jnp.where(sec == 0, pair[1], pair[0]), "section", pairs)
        return jnp.stack([jnp.where(sec == 0, own, other), jnp.where(sec == 0, other, own)])

    g_a, g_m, small = own_sum(grads_a), own_sum(grads_m), own_sum(smalls)
    split = jnp.concatenate([g_a[:, : 2 * hd], g_m], axis=1).astype(BF)
    split = lax.psum_scatter(split, "dp", scatter_dimension=0, tiled=True).astype(F32)
    kv, small = lax.psum((g_a[:, 2 * hd :], small), ("tensor", "dp"))
    return split[:, : 2 * hd], split[:, 2 * hd :], kv, small, placed(ys), placed(xs)


def per_device(tokens, segments, cotangent, *weights):
    nt, nd = lax.axis_size("tensor"), lax.axis_size("dp")
    sec = lax.axis_index("section")
    width = tokens.shape[1]
    hd = weights[1].shape[-1]
    units = weights[4].shape[-1]
    rows = MB_TOK
    x16 = lax.dynamic_slice_in_dim(tokens, sec * rows, rows, 0)
    cot = lax.dynamic_slice_in_dim(cotangent, sec * rows, rows, 0)
    seg = lax.dynamic_slice_in_dim(segments, sec * rows, rows, 0)
    w0, w1 = both_layers(weights)
    at = jnp.arange(rows, dtype=jnp.int32)
    seen = (seg[:, None] == seg[None, :]) & (at[None, :] <= at[:, None])
    position = (jnp.sum(seen.astype(jnp.int32), axis=1) - 1).astype(F32)
    freq = jnp.exp(jnp.arange(hd // 2, dtype=F32) * (-2.0 * math.log(10000.0) / hd))
    angles = position[:, None] * freq[None, :]
    tables = (jnp.cos(angles), jnp.sin(angles), seg[:, None], seg[None, :])

    n2_0, *kept_0, att_0, res_0 = attend_forward(x16, w0, tables, nt, 3)
    y_0, gate_0, up_0, h_0, mlp_0 = feed_forward(n2_0, res_0, w0, None, nt, 4)
    n2_1, *kept_1, att_1, res_1 = attend_forward(y_0, w1, tables, nt, 3)
    y_1, d_mlp_1, gate_1, up_1, h_1, _, dg3_1 = feed_forward(n2_1, res_1, w1, cot, nt, 5)

    d_att_1, gm_1, dr_1, dg1_1, dg2_1, _, _ = feed_backward(
        d_mlp_1, cot, (n2_1, gate_1, up_1, h_1, res_1, att_1), w1, nt, 6
    )
    dx_1, d_mlp_0, ga_1, dg0_1, dgq_1, dgk_1, _, _, _, dg3_0 = attend_backward(
        d_att_1, dr_1, y_0, kept_1, w1, tables, (mlp_0, w0[7]), nt, 7
    )
    d_att_0, gm_0, dr_0, dg1_0, dg2_0, _, _ = feed_backward(
        d_mlp_0, dx_1, (n2_0, gate_0, up_0, h_0, res_0, att_0), w0, nt, 6
    )
    dx_0, ga_0, dg0_0, dgq_0, dgk_0, _, _, _ = attend_backward(
        d_att_0, dr_0, x16, kept_0, w0, tables, None, nt, 8
    )

    def small(g0, g1, g2, g3, q, k):
        tail = ((0, 2), (0, width - hd))
        return jnp.concatenate([g0, g1, g2, g3, jnp.pad(jnp.concatenate([q, k]), tail)])

    smalls = (
        small(dg0_0, dg1_0, dg2_0, dg3_0, dgq_0, dgk_0),
        small(dg0_1, dg1_1, dg2_1, dg3_1, dgq_1, dgk_1),
    )
    fits = width % (16 * nd) == 0 and (2 * hd // nt) % 128 == 0 and nt * nd <= 32
    reducer = reduce_all if fits else reduce_plain
    g_a, g_m, kv, sums, out_y, out_x = reducer(
        (ga_0, ga_1), (gm_0, gm_1), smalls, (y_0, y_1), (dx_0, dx_1), nt, nd, hd
    )
    if fits:
        kv = kv.reshape(nd, nt, width // nd, 2 * hd // nt).transpose(0, 2, 1, 3).reshape(width, 2 * hd)
        kv = kv.astype(F32)
    cols = width // nd
    gains = lax.dynamic_slice(sums, (0, lax.axis_index("dp") * cols), (4, cols))
    return (
        out_y.astype(F32).reshape(1, 2 * rows, width),
        out_x.astype(F32).reshape(1, 2 * rows, width),
        g_a[None, :, :hd],
        kv[None, :, :hd],
        kv[None, :, hd:],
        g_a[:, hd:].T[None],
        g_m[None, :, :units],
        g_m[None, :, units : 2 * units],
        g_m[:, 2 * units :].T[None],
        gains[None],
        sums[None, 4:6, :hd],
    )


def solution(mesh):
    return jax.shard_map(
        per_device,
        mesh=mesh,
        in_specs=(
            P("dp", None),
            P("dp"),
            P("dp", None),
            P("section", None, "tensor"),
            P("section", None, None),
            P("section", None, None),
            P("section", "tensor", None),
            P("section", None, "tensor"),
            P("section", None, "tensor"),
            P("section", "tensor", None),
            P("section", None, None),
            P("section", None, None),
        ),
        out_specs=(
            P("section", "dp", None),
            P("section", "dp", None),
            P("section", "dp", "tensor"),
            P("section", None, None),
            P("section", None, None),
            P("section", "tensor", "dp"),
            P("section", "dp", "tensor"),
            P("section", "dp", "tensor"),
            P("section", "tensor", "dp"),
            P("section", None, "dp"),
            P("section", None, None),
        ),
        check_vma=False,
    )
```

```python
import functools
import math

import jax
import jax.numpy as jnp
from jax import lax
from jax.experimental import pallas as pl
from jax.experimental.pallas import tpu as pltpu
from jax.sharding import PartitionSpec as P

WINDOW = 512
MB_TOK = 256
EPSILON = 1e-06
BF = jnp.bfloat16
F32 = jnp.float32
MESH = pl.DeviceIdType.MESH
VM = pl.BlockSpec(memory_space=pltpu.VMEM)
VMEM_LIMIT = 50 * 1024 * 1024


def mm(a, b):
    return lax.dot_general(a, b, (((1,), (0,)), ((), ())), preferred_element_type=F32)


def mm_t(a, b):
    return lax.dot_general(a, b, (((1,), (1,)), ((), ())), preferred_element_type=F32)


def t_mm(a, b):
    return lax.dot_general(a, b, (((0,), (0,)), ((), ())), preferred_element_type=F32)


def inverse_rms(v):
    return lax.rsqrt(jnp.mean(v * v, axis=-1, keepdims=True) + EPSILON)


def rms(v):
    return v * inverse_rms(v)


def rms_back(v, gain, cot):
    inv = inverse_rms(v)
    unit = v * inv
    weighted = cot * gain
    d_v = inv * (weighted - unit * jnp.mean(weighted * unit, axis=-1, keepdims=True))
    return d_v, jnp.sum(cot * unit, axis=0, keepdims=True)


def rope(u, cos, sin):
    half = u.shape[-1] // 2
    a, b = u[:, :half], u[:, half:]
    return jnp.concatenate([a * cos - b * sin, b * cos + a * sin], axis=-1)


def rope_back(d, cos, sin):
    half = d.shape[-1] // 2
    a, b = d[:, :half], d[:, half:]
    return jnp.concatenate([a * cos + b * sin, b * cos - a * sin], axis=-1)


GELU_C = math.sqrt(2.0 / math.pi)


def gelu_parts(g):
    th = jnp.tanh(GELU_C * (g + 0.044715 * g * g * g))
    value = 0.5 * g * (1.0 + th)
    slope = 0.5 * (1.0 + th) + 0.5 * g * (1.0 - th * th) * GELU_C * (1.0 + 3 * 0.044715 * g * g)
    return value, slope


def call_exchange(ins, out_shapes, gathered, pre, during, shard, ranks, collective_id):
    n_in, n_out = len(ins), len(out_shapes)
    rows, width = MB_TOK, ins[0].shape[-1]
    share = rows // ranks

    def kernel(*refs):
        in_refs = refs[:n_in]
        gat = refs[n_in : n_in + gathered]
        outs = refs[n_in + gathered : n_in + gathered + n_out]
        part, recv, rs_send, rs_recv, ag_send, ag_recv = refs[n_in + gathered + n_out :]
        me = lax.axis_index("tensor")
        peers = [lax.rem(me + d, ranks) for d in range(1, ranks)]
        barrier = pltpu.get_barrier_semaphore()
        for peer in peers:
            pl.semaphore_signal(barrier, inc=1, device_id={"tensor": peer}, device_id_type=MESH)
        own = pl.ds(pl.multiple_of(me * share, share), share)
        part[...] = pre(in_refs, outs).astype(BF)
        pl.semaphore_wait(barrier, ranks - 1)
        copies = []
        for d, peer in enumerate(peers):
            copy = pltpu.make_async_remote_copy(
                src_ref=part.at[pl.ds(pl.multiple_of(peer * share, share), share)],
                dst_ref=recv.at[d],
                send_sem=rs_send.at[d],
                recv_sem=rs_recv.at[d],
                device_id={"tensor": peer},
                device_id_type=MESH,
            )
            copy.start()
            copies.append(copy)
        if during is not None:
            during(in_refs, outs)
        total = part[own].astype(F32)
        for d, copy in enumerate(copies):
            copy.wait_recv()
            total = total + recv[d].astype(F32)
        results = shard(total, own, in_refs, outs)
        sends = []
        for i in range(gathered):
            gat[i][own] = results[i]
            for d, peer in enumerate(peers):
                copy = pltpu.make_async_remote_copy(
                    src_ref=gat[i].at[own],
                    dst_ref=gat[i].at[own],
                    send_sem=ag_send.at[i, d],
                    recv_sem=ag_recv.at[i, d],
                    device_id={"tensor": peer},
                    device_id_type=MESH,
                )
                copy.start()
                sends.append(copy)
        for copy in copies:
            copy.wait_send()
        for copy in sends:
            copy.wait()

    return pl.pallas_call(
        kernel,
        out_shape=[jax.ShapeDtypeStruct((rows, width), BF)] * gathered + out_shapes,
        in_specs=[VM] * n_in,
        out_specs=[VM] * (gathered + n_out),
        scratch_shapes=[
            pltpu.VMEM((rows, width), BF),
            pltpu.VMEM((ranks - 1, share, width), BF),
            pltpu.SemaphoreType.DMA((ranks - 1,)),
            pltpu.SemaphoreType.DMA((ranks - 1,)),
            pltpu.SemaphoreType.DMA((gathered, ranks - 1)),
            pltpu.SemaphoreType.DMA((gathered, ranks - 1)),
        ],
        compiler_params=pltpu.CompilerParams(
            collective_id=collective_id, has_side_effects=True, vmem_limit_bytes=VMEM_LIMIT
        ),
    )(*ins)


def swap_kernel(count, *refs):
    ins, firsts, seconds = refs[:count], refs[count : 2 * count], refs[2 * count : 3 * count]
    local_sem, send_sem, recv_sem = refs[3 * count :]
    me = lax.axis_index("section")
    other = 1 - me
    barrier = pltpu.get_barrier_semaphore()
    pl.semaphore_signal(barrier, inc=1, device_id={"section": other}, device_id_type=MESH)
    pl.semaphore_wait(barrier, 1)
    for sec, outs in ((0, firsts), (1, seconds)):

        @pl.when(me == sec)
        def _():
            copies = []
            for i in range(count):
                far = pltpu.make_async_remote_copy(
                    src_ref=ins[i],
                    dst_ref=outs[i],
                    send_sem=send_sem.at[i],
                    recv_sem=recv_sem.at[i],
                    device_id={"section": other},
                    device_id_type=MESH,
                )
                near = pltpu.make_async_copy(ins[i], outs[i], local_sem.at[i])
                far.start()
                near.start()
                copies += [far, near]
            for copy in copies:
                copy.wait()


def both_layers(weights):
    count = len(weights)
    shapes = [jax.ShapeDtypeStruct(w.shape, w.dtype) for w in weights]
    outs = pl.pallas_call(
        functools.partial(swap_kernel, count),
        out_shape=shapes * 2,
        in_specs=[VM] * count,
        out_specs=[VM] * (2 * count),
        scratch_shapes=[pltpu.SemaphoreType.DMA((count,))] * 3,
        compiler_params=pltpu.CompilerParams(
            collective_id=1, has_side_effects=True, vmem_limit_bytes=VMEM_LIMIT
        ),
    )(*weights)
    return outs[:count], outs[count:]


def struct(shape, dtype=F32):
    return jax.ShapeDtypeStruct(shape, dtype)


def attend_forward(x16, w, tables, ranks, cid):
    w_query, w_key, w_value, w_out, _, _, _, norm_gains, head_gains = w
    cos, sin, seg_col, seg_row = tables
    width = x16.shape[1]
    hd = w_key.shape[-1]
    rows = MB_TOK

    def pre(i, o):
        x_ref, wq, wk, wv, wo, ng, hg, cos, sin, sc, sr = i
        n1_o, qr_o, kr_o, q_o, k_o, v_o, p_o, mix_o = o[:8]
        n1 = (rms(x_ref[...].astype(F32)) * ng[0, 0:1]).astype(BF)
        n1_o[...] = n1
        qr = mm(n1, wq[0])
        kr = mm(n1, wk[0])
        v = mm(n1, wv[0]).astype(BF)
        qr_o[...] = qr
        kr_o[...] = kr
        v_o[...] = v
        q = rope(rms(qr) * hg[0, 0:1], cos[...], sin[...]).astype(BF)
        k = rope(rms(kr) * hg[0, 1:2], cos[...], sin[...]).astype(BF)
        q_o[...] = q
        k_o[...] = k
        at = lax.broadcasted_iota(jnp.int32, (rows, rows), 0)
        to = lax.broadcasted_iota(jnp.int32, (rows, rows), 1)
        allowed = (sc[...] == sr[...]) & (to <= at) & (at - to < WINDOW)
        s = jnp.where(allowed, mm_t(q, k) * (hd**-0.5), -1e30)
        e = jnp.exp(s - jnp.max(s, axis=-1, keepdims=True))
        p = e / jnp.sum(e, axis=-1, keepdims=True)
        p_o[...] = p
        mix = mm(p.astype(BF), v).astype(BF)
        mix_o[...] = mix
        return mm(mix, wo[0])

    def shard(total, own, i, o):
        ng = i[5]
        residual = i[0][own].astype(F32) + rms(total) * ng[0, 1:2]
        o[8][...] = total
        o[9][...] = residual
        return [(rms(residual) * ng[0, 2:3]).astype(BF)]

    share = rows // ranks
    return call_exchange(
        [x16, w_query, w_key, w_value, w_out, norm_gains, head_gains, cos, sin, seg_col, seg_row],
        [
            struct((rows, width), BF),
            struct((rows, hd)),
            struct((rows, hd)),
            struct((rows, hd), BF),
            struct((rows, hd), BF),
            struct((rows, hd), BF),
            struct((rows, rows)),
            struct((rows, hd), BF),
            struct((share, width)),
            struct((share, width)),
        ],
        1, pre, None, shard, ranks, cid,
    )


def feed_forward(n2, residual, w, cot, ranks, cid):
    _, _, _, _, w_gate, w_up, w_down, norm_gains, _ = w
    width = n2.shape[1]
    units = w_gate.shape[-1]
    rows = MB_TOK
    share = rows // ranks

    def pre(i, o):
        n2_ref, res, wg, wu, wd, ng = i[:6]
        n2 = n2_ref[...]
        gate = mm(n2, wg[0])
        up = mm(n2, wu[0])
        h = (gelu_parts(gate)[0] * up).astype(BF)
        o[0][...] = gate
        o[1][...] = up
        o[2][...] = h
        return mm(h, wd[0])

    def shard(total, own, i, o):
        res, ng = i[1], i[5]
        gain = ng[0, 3:4]
        y16 = (res[...] + rms(total) * gain).astype(BF)
        o[3][...] = total
        if cot is None:
            return [y16]
        d_mlp, d_gain = rms_back(total, gain, i[6][own].astype(F32))
        o[4][...] = d_gain
        return [y16, d_mlp.astype(BF)]

    outs = [struct((rows, units)), struct((rows, units)), struct((rows, units), BF), struct((share, width))]
    ins = [n2, residual, w_gate, w_up, w_down, norm_gains]
    if cot is not None:
        ins.append(cot)
        outs.append(struct((1, width)))
    return call_exchange(ins, outs, 1 if cot is None else 2, pre, None, shard, ranks, cid)


def feed_backward(d_mlp16, dy16, kept, w, ranks, cid):
    _, _, _, _, w_gate, w_up, w_down, norm_gains, _ = w
    n2, gate, up, h, residual, attended = kept
    width = n2.shape[1]
    units = w_gate.shape[-1]
    rows = MB_TOK
    share = rows // ranks

    def pre(i, o):
        dm, _, _, gate, up, _, _, _, wg, wu, wd, _ = i
        dh = mm_t(dm[...], wd[0])
        value, slope = gelu_parts(gate[...])
        dg = (dh * up[...] * slope).astype(BF)
        du = (dh * value).astype(BF)
        o[4][...] = dg
        o[5][...] = du
        return mm_t(dg, wg[0]) + mm_t(du, wu[0])

    def during(i, o):
        dm, n2, h = i[0], i[2], i[5]
        o[0][:, :units] = t_mm(n2[...], o[4][...]).astype(BF)
        o[0][:, units : 2 * units] = t_mm(n2[...], o[5][...]).astype(BF)
        o[0][:, 2 * units :] = t_mm(dm[...], h[...]).astype(BF)

    def shard(total, own, i, o):
        dy, res, att, ng = i[1], i[6], i[7], i[11]
        d_branch, dg2 = rms_back(res[...], ng[0, 2:3], total)
        dr = dy[own].astype(F32) + d_branch
        d_att, dg1 = rms_back(att[...], ng[0, 1:2], dr)
        o[1][...] = dr
        o[2][...] = dg1
        o[3][...] = dg2
        return [d_att.astype(BF)]

    return call_exchange(
        [d_mlp16, dy16, n2, gate, up, h, residual, attended, w_gate, w_up, w_down, norm_gains],
        [
            struct((width, 3 * units), BF),
            struct((share, width)),
            struct((1, width)),
            struct((1, width)),
            struct((rows, units), BF),
            struct((rows, units), BF),
        ],
        1, pre, during, shard, ranks, cid,
    )


def attend_backward(d_att16, dr, x16, kept, w, tables, below, ranks, cid):
    w_query, w_key, w_value, w_out, _, _, _, norm_gains, head_gains = w
    n1, qr, kr, q, k, v, p, mix = kept
    cos, sin = tables[:2]
    width = n1.shape[1]
    hd = w_key.shape[-1]
    rows = MB_TOK

    def pre(i, o):
        da, _, _, n1, qr, kr, q, k, v, p, mix, cos, sin, wq, wk, wv, wo, _, hg = i[:19]
        scale = hd**-0.5
        do = mm_t(da[...], wo[0]).astype(BF)
        p = p[...]
        d_p = mm_t(do, v[...])
        ds = (p * (d_p - jnp.sum(p * d_p, axis=-1, keepdims=True))).astype(BF)
        dq = mm(ds, k[...]) * scale
        dk = t_mm(ds, q[...]) * scale
        dv = t_mm(p.astype(BF), do).astype(BF)
        dq_raw, dgq = rms_back(qr[...], hg[0, 0:1], rope_back(dq, cos[...], sin[...]))
        dk_raw, dgk = rms_back(kr[...], hg[0, 1:2], rope_back(dk, cos[...], sin[...]))
        dq_raw = dq_raw.astype(BF)
        dk_raw = dk_raw.astype(BF)
        o[2][...] = dgq
        o[3][...] = dgk
        o[4][...] = dq_raw
        o[5][...] = dk_raw
        o[6][...] = dv
        return mm_t(dq_raw, wq[0]) + mm_t(dk_raw, wk[0]) + mm_t(dv, wv[0])

    def during(i, o):
        da, n1, mix = i[0][...], i[3][...], i[10][...]
        o[0][:, :hd] = t_mm(n1, o[4][...]).astype(BF)
        o[0][:, hd : 2 * hd] = t_mm(da, mix).astype(BF)
        o[0][:, 2 * hd : 3 * hd] = t_mm(n1, o[5][...]).astype(BF)
        o[0][:, 3 * hd :] = t_mm(n1, o[6][...]).astype(BF)

    def shard(total, own, i, o):
        d_branch, dg0 = rms_back(i[2][own].astype(F32), i[17][0, 0:1], total)
        o[1][...] = dg0
        dx16 = (i[1][...] + d_branch).astype(BF)
        if below is None:
            return [dx16]
        d_mlp, dg3 = rms_back(i[19][...], i[20][0, 3:4], dx16.astype(F32))
        o[7][...] = dg3
        return [dx16, d_mlp.astype(BF)]

    ins = [d_att16, dr, x16, n1, qr, kr, q, k, v, p, mix, cos, sin]
    ins += [w_query, w_key, w_value, w_out, norm_gains, head_gains]
    outs = [
        struct((width, 4 * hd), BF),
        struct((1, width)),
        struct((1, hd)),
        struct((1, hd)),
        struct((rows, hd), BF),
        struct((rows, hd), BF),
        struct((rows, hd), BF),
    ]
    if below is not None:
        ins += list(below)
        outs.append(struct((1, width)))
    return call_exchange(ins, outs, 1 if below is None else 2, pre, during, shard, ranks, cid)


def reduce_kernel(nt, nd, hd, *refs):
    (ga0, ga1, gm0, gm1, s0, s1, y0, y1, x0, x1) = refs[:10]
    (out_a, out_m, out_kv, out_s, out_y, out_x) = refs[10:16]
    (swap_a, swap_m, swap_s, h_a, h_m, r_a, r_m, kv_part, kv_recv, s_sum, s_recv) = refs[16:27]
    (sw_send, sw_recv, sm_send, sm_recv, lo_sem, dp_send, dp_recv, kt_send, kt_recv) = refs[27:36]
    (ka_send, ka_recv, ss_send, ss_recv) = refs[36:]
    sec = lax.axis_index("section")
    t = lax.axis_index("tensor")
    z = lax.axis_index("dp")
    total = nt * nd
    me = z * nt + t
    rows = ga0.shape[0] // nd
    section = {"section": 1 - sec}
    group = []
    for step in range(1, total):
        flat = lax.rem(me + step, total)
        group.append({"dp": flat // nt, "tensor": lax.rem(flat, nt)})
    barrier = pltpu.get_barrier_semaphore()
    for device in [section] + group:
        pl.semaphore_signal(barrier, inc=1, device_id=device, device_id_type=MESH)
    pl.semaphore_wait(barrier, total)

    def remote(src, dst, send, recv, device):
        return pltpu.make_async_remote_copy(
            src_ref=src, dst_ref=dst, send_sem=send, recv_sem=recv,
            device_id=device, device_id_type=MESH,
        )

    zs = [lax.rem(z + d, nd) for d in range(1, nd)] + [z]
    spans = [pl.ds(pl.multiple_of(peer * rows, rows), rows) for peer in zs]

    def swap(ga, gm, s, y, x):
        first = [remote(s, swap_s, sm_send.at[0], sm_recv.at[0], section)]
        for n, span in enumerate(spans):
            first.append(remote(ga.at[span], swap_a.at[span], sw_send.at[0, n], sw_recv.at[0, n], section))
        for n, span in enumerate(spans):
            first.append(remote(gm.at[span], swap_m.at[span], sw_send.at[1, n], sw_recv.at[1, n], section))
        first.append(remote(y, out_y.at[sec], sm_send.at[1], sm_recv.at[1], section))
        first.append(remote(x, out_x.at[sec], sm_send.at[2], sm_recv.at[2], section))
        return first

    @pl.when(sec == 0)
    def _():
        for copy in swap(ga1, gm1, s1, y1, x1):
            copy.start()
        pltpu.make_async_copy(y0, out_y.at[0], lo_sem.at[0]).start()
        pltpu.make_async_copy(x0, out_x.at[0], lo_sem.at[1]).start()

    @pl.when(sec == 1)
    def _():
        for copy in swap(ga0, gm0, s0, y0, x0):
            copy.start()
        pltpu.make_async_copy(y1, out_y.at[1], lo_sem.at[0]).start()
        pltpu.make_async_copy(x1, out_x.at[1], lo_sem.at[1]).start()

    waits = swap(ga0, gm0, s0, y0, x0)
    waits[0].wait_recv()

    @pl.when(sec == 0)
    def _():
        s_sum[...] = s0[...] + swap_s[...]

    @pl.when(sec == 1)
    def _():
        s_sum[...] = s1[...] + swap_s[...]

    s_copies = []
    for step, device in enumerate(group):
        copy = remote(s_sum, s_recv.at[step], ss_send.at[step], ss_recv.at[step], device)
        copy.start()
        s_copies.append(copy)
    dp_copies = []
    for kind, (g_0, g_1, got, held, landed) in enumerate(
        ((ga0, ga1, swap_a, h_a, r_a), (gm0, gm1, swap_m, h_m, r_m))
    ):
        for n in range(nd):
            waits[1 + kind * nd + n].wait_recv()
            span = spans[n]

            @pl.when(sec == 0)
            def _():
                held[n] = (g_0[span].astype(F32) + got[span].astype(F32)).astype(BF)

            @pl.when(sec == 1)
            def _():
                held[n] = (g_1[span].astype(F32) + got[span].astype(F32)).astype(BF)

            if n < nd - 1:
                copy = remote(
                    held.at[n], landed.at[n], dp_send.at[kind, n], dp_recv.at[kind, n], {"dp": zs[n]}
                )
                copy.start()
                dp_copies.append(copy)
    for n in range(nd - 1):
        dp_copies[n].wait_recv()
    acc = h_a[nd - 1].astype(F32)
    for n in range(nd - 1):
        acc = acc + r_a[n].astype(F32)
    out_a[...] = acc[:, : 2 * hd]
    piece = 2 * hd // nt
    for n in range(nt):
        kv_part[n] = acc[:, 2 * hd + n * piece : 2 * hd + (n + 1) * piece].astype(BF)
    kt_copies = []
    for d in range(1, nt):
        peer = lax.rem(t + d, nt)
        copy = remote(
            kv_part.at[peer], kv_recv.at[d - 1], kt_send.at[d - 1], kt_recv.at[d - 1], {"tensor": peer}
        )
        copy.start()
        kt_copies.append(copy)
    mine = kv_part[t].astype(F32)
    for d, copy in enumerate(kt_copies):
        copy.wait_recv()
        mine = mine + kv_recv[d].astype(F32)
    out_kv[me] = mine.astype(BF)
    ka_copies = []
    for step, device in enumerate(group):
        copy = remote(out_kv.at[me], out_kv.at[me], ka_send.at[step], ka_recv.at[step], device)
        copy.start()
        ka_copies.append(copy)
    acc_s = s_sum[...]
    for step, copy in enumerate(s_copies):
        copy.wait_recv()
        acc_s = acc_s + s_recv[step]
    out_s[...] = acc_s
    for n in range(nd - 1):
        dp_copies[nd - 1 + n].wait_recv()
    acc_m = h_m[nd - 1].astype(F32)
    for n in range(nd - 1):
        acc_m = acc_m + r_m[n].astype(F32)
    out_m[...] = acc_m
    waits[-2].wait_recv()
    waits[-1].wait_recv()
    pltpu.make_async_copy(y0, out_y.at[sec], lo_sem.at[0]).wait()
    pltpu.make_async_copy(x0, out_x.at[sec], lo_sem.at[1]).wait()
    for copy in ka_copies:
        copy.wait()
    for copy in waits + s_copies + dp_copies + kt_copies:
        copy.wait_send()


def reduce_all(grads_a, grads_m, smalls, ys, xs, nt, nd, hd):
    width, wa = grads_a[0].shape
    wm = grads_m[0].shape[1]
    rows = width // nd
    total = nt * nd
    dma = pltpu.SemaphoreType.DMA
    ins = list(grads_a) + list(grads_m) + list(smalls) + list(ys) + list(xs)
    tok = ys[0].shape
    return pl.pallas_call(
        functools.partial(reduce_kernel, nt, nd, hd),
        out_shape=[
            struct((rows, 2 * hd)),
            struct((rows, wm)),
            struct((total, rows, 2 * hd // nt), BF),
            struct(smalls[0].shape),
            struct((2,) + tok, BF),
            struct((2,) + tok, BF),
        ],
        in_specs=[VM] * len(ins),
        out_specs=[VM] * 6,
        scratch_shapes=[
            pltpu.VMEM((width, wa), BF),
            pltpu.VMEM((width, wm), BF),
            pltpu.VMEM(smalls[0].shape, F32),
            pltpu.VMEM((nd, rows, wa), BF),
            pltpu.VMEM((nd, rows, wm), BF),
            pltpu.VMEM((nd - 1, rows, wa), BF),
            pltpu.VMEM((nd - 1, rows, wm), BF),
            pltpu.VMEM((nt, rows, 2 * hd // nt), BF),
            pltpu.VMEM((nt - 1, rows, 2 * hd // nt), BF),
            pltpu.VMEM(smalls[0].shape, F32),
            pltpu.VMEM((total - 1,) + smalls[0].shape, F32),
            dma((2, nd)), dma((2, nd)), dma((3,)), dma((3,)), dma((2,)),
            dma((2, nd - 1)), dma((2, nd - 1)), dma((nt - 1,)), dma((nt - 1,)),
            dma((total - 1,)), dma((total - 1,)), dma((total - 1,)), dma((total - 1,)),
        ],
        compiler_params=pltpu.CompilerParams(
            collective_id=2, has_side_effects=True, vmem_limit_bytes=VMEM_LIMIT
        ),
    )(*ins)


def reduce_plain(grads_a, grads_m, smalls, ys, xs, nt, nd, hd):
    sec = lax.axis_index("section")
    pairs = [(0, 1), (1, 0)]

    def own_sum(pair):
        own = jnp.where(sec == 0, pair[0], pair[1])
        other = jnp.where(sec == 0, pair[1], pair[0])
        return own.astype(F32) + lax.ppermute(other, "section", pairs).astype(F32)

    def placed(pair):
        own = jnp.where(sec == 0, pair[0], pair[1])
        other = lax.ppermute(jnp.where(sec == 0, pair[1], pair[0]), "section", pairs)
        return jnp.stack([jnp.where(sec == 0, own, other), jnp.where(sec == 0, other, own)])

    g_a, g_m, small = own_sum(grads_a), own_sum(grads_m), own_sum(smalls)
    split = jnp.concatenate([g_a[:, : 2 * hd], g_m], axis=1).astype(BF)
    split = lax.psum_scatter(split, "dp", scatter_dimension=0, tiled=True).astype(F32)
    kv, small = lax.psum((g_a[:, 2 * hd :], small), ("tensor", "dp"))
    return split[:, : 2 * hd], split[:, 2 * hd :], kv, small, placed(ys), placed(xs)


def per_device(tokens, segments, cotangent, *weights):
    nt, nd = lax.axis_size("tensor"), lax.axis_size("dp")
    sec = lax.axis_index("section")
    width = tokens.shape[1]
    hd = weights[1].shape[-1]
    units = weights[4].shape[-1]
    rows = MB_TOK
    x16 = lax.dynamic_slice_in_dim(tokens, sec * rows, rows, 0)
    cot = lax.dynamic_slice_in_dim(cotangent, sec * rows, rows, 0)
    seg = lax.dynamic_slice_in_dim(segments, sec * rows, rows, 0)
    w0, w1 = both_layers(weights)
    at = jnp.arange(rows, dtype=jnp.int32)
    seen = (seg[:, None] == seg[None, :]) & (at[None, :] <= at[:, None])
    position = (jnp.sum(seen.astype(jnp.int32), axis=1) - 1).astype(F32)
    freq = jnp.exp(jnp.arange(hd // 2, dtype=F32) * (-2.0 * math.log(10000.0) / hd))
    angles = position[:, None] * freq[None, :]
    tables = (jnp.cos(angles), jnp.sin(angles), seg[:, None], seg[None, :])

    n2_0, *kept_0, att_0, res_0 = attend_forward(x16, w0, tables, nt, 3)
    y_0, gate_0, up_0, h_0, mlp_0 = feed_forward(n2_0, res_0, w0, None, nt, 4)
    n2_1, *kept_1, att_1, res_1 = attend_forward(y_0, w1, tables, nt, 3)
    y_1, d_mlp_1, gate_1, up_1, h_1, _, dg3_1 = feed_forward(n2_1, res_1, w1, cot, nt, 5)

    d_att_1, gm_1, dr_1, dg1_1, dg2_1, _, _ = feed_backward(
        d_mlp_1, cot, (n2_1, gate_1, up_1, h_1, res_1, att_1), w1, nt, 6
    )
    dx_1, d_mlp_0, ga_1, dg0_1, dgq_1, dgk_1, _, _, _, dg3_0 = attend_backward(
        d_att_1, dr_1, y_0, kept_1, w1, tables, (mlp_0, w0[7]), nt, 7
    )
    d_att_0, gm_0, dr_0, dg1_0, dg2_0, _, _ = feed_backward(
        d_mlp_0, dx_1, (n2_0, gate_0, up_0, h_0, res_0, att_0), w0, nt, 6
    )
    dx_0, ga_0, dg0_0, dgq_0, dgk_0, _, _, _ = attend_backward(
        d_att_0, dr_0, x16, kept_0, w0, tables, None, nt, 8
    )

    def small(g0, g1, g2, g3, q, k):
        tail = ((0, 2), (0, width - hd))
        return jnp.concatenate([g0, g1, g2, g3, jnp.pad(jnp.concatenate([q, k]), tail)])

    smalls = (
        small(dg0_0, dg1_0, dg2_0, dg3_0, dgq_0, dgk_0),
        small(dg0_1, dg1_1, dg2_1, dg3_1, dgq_1, dgk_1),
    )
    fits = width % (16 * nd) == 0 and (2 * hd // nt) % 128 == 0 and nt * nd <= 32
    reducer = reduce_all if fits else reduce_plain
    g_a, g_m, kv, sums, out_y, out_x = reducer(
        (ga_0, ga_1), (gm_0, gm_1), smalls, (y_0, y_1), (dx_0, dx_1), nt, nd, hd
    )
    if fits:
        kv = kv.reshape(nd, nt, width // nd, 2 * hd // nt).transpose(0, 2, 1, 3).reshape(width, 2 * hd)
        kv = kv.astype(F32)
    cols = width // nd
    gains = lax.dynamic_slice(sums, (0, lax.axis_index("dp") * cols), (4, cols))
    return (
        out_y.astype(F32).reshape(1, 2 * rows, width),
        out_x.astype(F32).reshape(1, 2 * rows, width),
        g_a[None, :, :hd],
        kv[None, :, :hd],
        kv[None, :, hd:],
        g_a[:, hd:].T[None],
        g_m[None, :, :units],
        g_m[None, :, units : 2 * units],
        g_m[:, 2 * units :].T[None],
        gains[None],
        sums[None, 4:6, :hd],
    )


def solution(mesh):
    return jax.shard_map(
        per_device,
        mesh=mesh,
        in_specs=(
            P("dp", None),
            P("dp"),
            P("dp", None),
            P("section", None, "tensor"),
            P("section", None, None),
            P("section", None, None),
            P("section", "tensor", None),
            P("section", None, "tensor"),
            P("section", None, "tensor"),
            P("section", "tensor", None),
            P("section", None, None),
            P("section", None, None),
        ),
        out_specs=(
            P("section", "dp", None),
            P("section", "dp", None),
            P("section", "dp", "tensor"),
            P("section", None, None),
            P("section", None, None),
            P("section", "tensor", "dp"),
            P("section", "dp", "tensor"),
            P("section", "dp", "tensor"),
            P("section", "tensor", "dp"),
            P("section", None, "dp"),
            P("section", None, None),
        ),
        check_vma=False,
    )
```

```python
import functools
import math

import jax
import jax.numpy as jnp
from jax import lax
from jax.experimental import pallas as pl
from jax.experimental.pallas import tpu as pltpu
from jax.sharding import PartitionSpec as P

WINDOW = 512
MB_TOK = 256
EPSILON = 1e-06
BF = jnp.bfloat16
F32 = jnp.float32
MESH = pl.DeviceIdType.MESH
VM = pl.BlockSpec(memory_space=pltpu.VMEM)
VMEM_LIMIT = 50 * 1024 * 1024


def mm(a, b):
    return lax.dot_general(a, b, (((1,), (0,)), ((), ())), preferred_element_type=F32)


def mm_t(a, b):
    return lax.dot_general(a, b, (((1,), (1,)), ((), ())), preferred_element_type=F32)


def t_mm(a, b):
    return lax.dot_general(a, b, (((0,), (0,)), ((), ())), preferred_element_type=F32)


def inverse_rms(v):
    return lax.rsqrt(jnp.mean(v * v, axis=-1, keepdims=True) + EPSILON)


def rms(v):
    return v * inverse_rms(v)


def rms_back(v, gain, cot):
    inv = inverse_rms(v)
    unit = v * inv
    weighted = cot * gain
    d_v = inv * (weighted - unit * jnp.mean(weighted * unit, axis=-1, keepdims=True))
    return d_v, jnp.sum(cot * unit, axis=0, keepdims=True)


def rope(u, cos, sin):
    half = u.shape[-1] // 2
    a, b = u[:, :half], u[:, half:]
    return jnp.concatenate([a * cos - b * sin, b * cos + a * sin], axis=-1)


def rope_back(d, cos, sin):
    half = d.shape[-1] // 2
    a, b = d[:, :half], d[:, half:]
    return jnp.concatenate([a * cos + b * sin, b * cos - a * sin], axis=-1)


GELU_C = math.sqrt(2.0 / math.pi)


def gelu_parts(g):
    th = jnp.tanh(GELU_C * (g + 0.044715 * g * g * g))
    value = 0.5 * g * (1.0 + th)
    slope = 0.5 * (1.0 + th) + 0.5 * g * (1.0 - th * th) * GELU_C * (1.0 + 3 * 0.044715 * g * g)
    return value, slope


class GradSum:
    def __init__(self, nd, grad):
        self.nd = nd
        self.half = grad.shape[0] // (2 * nd)
        self.width = grad.shape[1]

    def scratch(self):
        dma = pltpu.SemaphoreType.DMA
        block = (self.half, self.width)
        return [
            pltpu.VMEM((self.nd,) + block, BF),
            pltpu.VMEM((self.nd,) + block, BF),
            pltpu.VMEM((self.nd - 1,) + block, BF),
            dma((self.nd,)), dma((self.nd,)), dma((self.nd - 1,)), dma((self.nd - 1,)),
        ]

    def result(self):
        return struct((self.half, self.width))

    def devices(self):
        z = lax.axis_index("dp")
        peers = [{"dp": lax.rem(z + d, self.nd)} for d in range(1, self.nd)]
        return [{"section": 1 - lax.axis_index("section")}] + peers

    def begin(self, grad, refs):
        self.grad = grad
        self.got, self.held, self.landed, sw_send, sw_recv, self.dp_send, self.dp_recv = refs
        sec, z = lax.axis_index("section"), lax.axis_index("dp")
        self.zs = [lax.rem(z + d, self.nd) for d in range(1, self.nd)] + [z]
        self.swaps = []
        for n, peer in enumerate(self.zs):
            copy = pltpu.make_async_remote_copy(
                src_ref=grad.at[self.rows(peer, 1 - sec)],
                dst_ref=self.got.at[n],
                send_sem=sw_send.at[n],
                recv_sem=sw_recv.at[n],
                device_id={"section": 1 - sec},
                device_id_type=MESH,
            )
            copy.start()
            self.swaps.append(copy)

    def rows(self, peer, core):
        return pl.ds(pl.multiple_of((2 * peer + core) * self.half, self.half), self.half)

    def send(self):
        sec = lax.axis_index("section")
        self.sends = []
        for n, peer in enumerate(self.zs):
            self.swaps[n].wait_recv()
            own = self.grad[self.rows(peer, sec)].astype(F32)
            self.held[n] = (own + self.got[n].astype(F32)).astype(BF)
            if n < self.nd - 1:
                copy = pltpu.make_async_remote_copy(
                    src_ref=self.held.at[n],
                    dst_ref=self.landed.at[n],
                    send_sem=self.dp_send.at[n],
                    recv_sem=self.dp_recv.at[n],
                    device_id={"dp": peer},
                    device_id_type=MESH,
                )
                copy.start()
                self.sends.append(copy)

    def finish(self):
        total = self.held[self.nd - 1].astype(F32)
        for n, copy in enumerate(self.sends):
            copy.wait_recv()
            total = total + self.landed[n].astype(F32)
        for copy in self.swaps + self.sends:
            copy.wait_send()
        return total


def call_exchange(ins, out_shapes, gathered, pre, during, shard, ranks, collective_id, behind=None):
    job = None
    if behind is not None:
        job = GradSum(lax.axis_size("dp"), behind)
        ins = ins + [behind]
        out_shapes = out_shapes + [job.result()]
    n_in, n_out = len(ins), len(out_shapes)
    rows, width = MB_TOK, ins[0].shape[-1]
    share = rows // ranks

    def kernel(*refs):
        in_refs = refs[:n_in]
        gat = refs[n_in : n_in + gathered]
        outs = refs[n_in + gathered : n_in + gathered + n_out]
        scratch = refs[n_in + gathered + n_out :]
        part, recv, rs_send, rs_recv, ag_send, ag_recv = scratch[:6]
        me = lax.axis_index("tensor")
        peers = [lax.rem(me + d, ranks) for d in range(1, ranks)]
        barrier = pltpu.get_barrier_semaphore()
        devices = [{"tensor": peer} for peer in peers] + (job.devices() if job else [])
        for device in devices:
            pl.semaphore_signal(barrier, inc=1, device_id=device, device_id_type=MESH)
        own = pl.ds(pl.multiple_of(me * share, share), share)
        if job:
            pl.semaphore_wait(barrier, len(devices))
            job.begin(in_refs[-1], scratch[6:])
        part[...] = pre(in_refs, outs).astype(BF)
        if not job:
            pl.semaphore_wait(barrier, len(devices))
        copies = []
        for d, peer in enumerate(peers):
            copy = pltpu.make_async_remote_copy(
                src_ref=part.at[pl.ds(pl.multiple_of(peer * share, share), share)],
                dst_ref=recv.at[d],
                send_sem=rs_send.at[d],
                recv_sem=rs_recv.at[d],
                device_id={"tensor": peer},
                device_id_type=MESH,
            )
            copy.start()
            copies.append(copy)
        if job:
            job.send()
        if during is not None:
            during(in_refs, outs)
        total = part[own].astype(F32)
        for d, copy in enumerate(copies):
            copy.wait_recv()
            total = total + recv[d].astype(F32)
        results = shard(total, own, in_refs, outs)
        sends = []
        for i in range(gathered):
            gat[i][own] = results[i]
            for d, peer in enumerate(peers):
                copy = pltpu.make_async_remote_copy(
                    src_ref=gat[i].at[own],
                    dst_ref=gat[i].at[own],
                    send_sem=ag_send.at[i, d],
                    recv_sem=ag_recv.at[i, d],
                    device_id={"tensor": peer},
                    device_id_type=MESH,
                )
                copy.start()
                sends.append(copy)
        for copy in copies:
            copy.wait_send()
        for copy in sends:
            copy.wait()
        if job:
            outs[-1][...] = job.finish()

    return pl.pallas_call(
        kernel,
        out_shape=[jax.ShapeDtypeStruct((rows, width), BF)] * gathered + out_shapes,
        in_specs=[VM] * n_in,
        out_specs=[VM] * (gathered + n_out),
        scratch_shapes=[
            pltpu.VMEM((rows, width), BF),
            pltpu.VMEM((ranks - 1, share, width), BF),
            pltpu.SemaphoreType.DMA((ranks - 1,)),
            pltpu.SemaphoreType.DMA((ranks - 1,)),
            pltpu.SemaphoreType.DMA((gathered, ranks - 1)),
            pltpu.SemaphoreType.DMA((gathered, ranks - 1)),
        ]
        + (job.scratch() if job else []),
        compiler_params=pltpu.CompilerParams(
            collective_id=collective_id, has_side_effects=True, vmem_limit_bytes=VMEM_LIMIT
        ),
    )(*ins)


def swap_kernel(count, *refs):
    ins, firsts, seconds = refs[:count], refs[count : 2 * count], refs[2 * count : 3 * count]
    local_sem, send_sem, recv_sem = refs[3 * count :]
    me = lax.axis_index("section")
    other = 1 - me
    barrier = pltpu.get_barrier_semaphore()
    pl.semaphore_signal(barrier, inc=1, device_id={"section": other}, device_id_type=MESH)
    pl.semaphore_wait(barrier, 1)
    for sec, outs in ((0, firsts), (1, seconds)):

        @pl.when(me == sec)
        def _():
            copies = []
            for i in range(count):
                far = pltpu.make_async_remote_copy(
                    src_ref=ins[i],
                    dst_ref=outs[i],
                    send_sem=send_sem.at[i],
                    recv_sem=recv_sem.at[i],
                    device_id={"section": other},
                    device_id_type=MESH,
                )
                near = pltpu.make_async_copy(ins[i], outs[i], local_sem.at[i])
                far.start()
                near.start()
                copies += [far, near]
            for copy in copies:
                copy.wait()


def both_layers(weights):
    count = len(weights)
    shapes = [jax.ShapeDtypeStruct(w.shape, w.dtype) for w in weights]
    outs = pl.pallas_call(
        functools.partial(swap_kernel, count),
        out_shape=shapes * 2,
        in_specs=[VM] * count,
        out_specs=[VM] * (2 * count),
        scratch_shapes=[pltpu.SemaphoreType.DMA((count,))] * 3,
        compiler_params=pltpu.CompilerParams(
            collective_id=1, has_side_effects=True, vmem_limit_bytes=VMEM_LIMIT
        ),
    )(*weights)
    return outs[:count], outs[count:]


def struct(shape, dtype=F32):
    return jax.ShapeDtypeStruct(shape, dtype)


def attend_forward(x16, w, tables, ranks, cid):
    w_query, w_key, w_value, w_out, _, _, _, norm_gains, head_gains = w
    cos, sin, seg_col, seg_row = tables
    width = x16.shape[1]
    hd = w_key.shape[-1]
    rows = MB_TOK

    def pre(i, o):
        x_ref, wq, wk, wv, wo, ng, hg, cos, sin, sc, sr = i
        n1_o, qr_o, kr_o, q_o, k_o, v_o, p_o, mix_o = o[:8]
        n1 = (rms(x_ref[...].astype(F32)) * ng[0, 0:1]).astype(BF)
        n1_o[...] = n1
        qr = mm(n1, wq[0])
        kr = mm(n1, wk[0])
        v = mm(n1, wv[0]).astype(BF)
        qr_o[...] = qr
        kr_o[...] = kr
        v_o[...] = v
        q = rope(rms(qr) * hg[0, 0:1], cos[...], sin[...]).astype(BF)
        k = rope(rms(kr) * hg[0, 1:2], cos[...], sin[...]).astype(BF)
        q_o[...] = q
        k_o[...] = k
        at = lax.broadcasted_iota(jnp.int32, (rows, rows), 0)
        to = lax.broadcasted_iota(jnp.int32, (rows, rows), 1)
        allowed = (sc[...] == sr[...]) & (to <= at) & (at - to < WINDOW)
        s = jnp.where(allowed, mm_t(q, k) * (hd**-0.5), -1e30)
        e = jnp.exp(s - jnp.max(s, axis=-1, keepdims=True))
        p = e / jnp.sum(e, axis=-1, keepdims=True)
        p_o[...] = p
        mix = mm(p.astype(BF), v).astype(BF)
        mix_o[...] = mix
        return mm(mix, wo[0])

    def shard(total, own, i, o):
        ng = i[5]
        residual = i[0][own].astype(F32) + rms(total) * ng[0, 1:2]
        o[8][...] = total
        o[9][...] = residual
        return [(rms(residual) * ng[0, 2:3]).astype(BF)]

    share = rows // ranks
    return call_exchange(
        [x16, w_query, w_key, w_value, w_out, norm_gains, head_gains, cos, sin, seg_col, seg_row],
        [
            struct((rows, width), BF),
            struct((rows, hd)),
            struct((rows, hd)),
            struct((rows, hd), BF),
            struct((rows, hd), BF),
            struct((rows, hd), BF),
            struct((rows, rows)),
            struct((rows, hd), BF),
            struct((share, width)),
            struct((share, width)),
        ],
        1, pre, None, shard, ranks, cid,
    )


def feed_forward(n2, residual, w, cot, ranks, cid):
    _, _, _, _, w_gate, w_up, w_down, norm_gains, _ = w
    width = n2.shape[1]
    units = w_gate.shape[-1]
    rows = MB_TOK
    share = rows // ranks

    def pre(i, o):
        n2_ref, res, wg, wu, wd, ng = i[:6]
        n2 = n2_ref[...]
        gate = mm(n2, wg[0])
        up = mm(n2, wu[0])
        h = (gelu_parts(gate)[0] * up).astype(BF)
        o[0][...] = gate
        o[1][...] = up
        o[2][...] = h
        return mm(h, wd[0])

    def shard(total, own, i, o):
        res, ng = i[1], i[5]
        gain = ng[0, 3:4]
        y16 = (res[...] + rms(total) * gain).astype(BF)
        o[3][...] = total
        if cot is None:
            return [y16]
        d_mlp, d_gain = rms_back(total, gain, i[6][own].astype(F32))
        o[4][...] = d_gain
        return [y16, d_mlp.astype(BF)]

    outs = [struct((rows, units)), struct((rows, units)), struct((rows, units), BF), struct((share, width))]
    ins = [n2, residual, w_gate, w_up, w_down, norm_gains]
    if cot is not None:
        ins.append(cot)
        outs.append(struct((1, width)))
    return call_exchange(ins, outs, 1 if cot is None else 2, pre, None, shard, ranks, cid)


def feed_backward(d_mlp16, dy16, kept, w, ranks, cid, behind=None):
    _, _, _, _, w_gate, w_up, w_down, norm_gains, _ = w
    n2, gate, up, h, residual, attended = kept
    width = n2.shape[1]
    units = w_gate.shape[-1]
    rows = MB_TOK
    share = rows // ranks

    def pre(i, o):
        dm, _, _, gate, up, _, _, _, wg, wu, wd, _ = i[:12]
        dh = mm_t(dm[...], wd[0])
        value, slope = gelu_parts(gate[...])
        dg = (dh * up[...] * slope).astype(BF)
        du = (dh * value).astype(BF)
        o[4][...] = dg
        o[5][...] = du
        return mm_t(dg, wg[0]) + mm_t(du, wu[0])

    def during(i, o):
        dm, n2, h = i[0], i[2], i[5]
        o[0][:, :units] = t_mm(n2[...], o[4][...]).astype(BF)
        o[0][:, units : 2 * units] = t_mm(n2[...], o[5][...]).astype(BF)
        o[0][:, 2 * units :] = t_mm(dm[...], h[...]).astype(BF)

    def shard(total, own, i, o):
        dy, res, att, ng = i[1], i[6], i[7], i[11]
        d_branch, dg2 = rms_back(res[...], ng[0, 2:3], total)
        dr = dy[own].astype(F32) + d_branch
        d_att, dg1 = rms_back(att[...], ng[0, 1:2], dr)
        o[1][...] = dr
        o[2][...] = dg1
        o[3][...] = dg2
        return [d_att.astype(BF)]

    return call_exchange(
        [d_mlp16, dy16, n2, gate, up, h, residual, attended, w_gate, w_up, w_down, norm_gains],
        [
            struct((width, 3 * units), BF),
            struct((share, width)),
            struct((1, width)),
            struct((1, width)),
            struct((rows, units), BF),
            struct((rows, units), BF),
        ],
        1, pre, during, shard, ranks, cid, behind,
    )


def attend_backward(d_att16, dr, x16, kept, w, tables, below, ranks, cid, behind=None):
    w_query, w_key, w_value, w_out, _, _, _, norm_gains, head_gains = w
    n1, qr, kr, q, k, v, p, mix = kept
    cos, sin = tables[:2]
    width = n1.shape[1]
    hd = w_key.shape[-1]
    rows = MB_TOK

    def pre(i, o):
        da, _, _, n1, qr, kr, q, k, v, p, mix, cos, sin, wq, wk, wv, wo, _, hg = i[:19]
        scale = hd**-0.5
        do = mm_t(da[...], wo[0]).astype(BF)
        p = p[...]
        d_p = mm_t(do, v[...])
        ds = (p * (d_p - jnp.sum(p * d_p, axis=-1, keepdims=True))).astype(BF)
        dq = mm(ds, k[...]) * scale
        dk = t_mm(ds, q[...]) * scale
        dv = t_mm(p.astype(BF), do).astype(BF)
        dq_raw, dgq = rms_back(qr[...], hg[0, 0:1], rope_back(dq, cos[...], sin[...]))
        dk_raw, dgk = rms_back(kr[...], hg[0, 1:2], rope_back(dk, cos[...], sin[...]))
        dq_raw = dq_raw.astype(BF)
        dk_raw = dk_raw.astype(BF)
        o[2][...] = dgq
        o[3][...] = dgk
        o[4][...] = dq_raw
        o[5][...] = dk_raw
        o[6][...] = dv
        return mm_t(dq_raw, wq[0]) + mm_t(dk_raw, wk[0]) + mm_t(dv, wv[0])

    def during(i, o):
        da, n1, mix = i[0][...], i[3][...], i[10][...]
        o[0][:, :hd] = t_mm(n1, o[4][...]).astype(BF)
        o[0][:, hd : 2 * hd] = t_mm(da, mix).astype(BF)
        o[0][:, 2 * hd : 3 * hd] = t_mm(n1, o[5][...]).astype(BF)
        o[0][:, 3 * hd :] = t_mm(n1, o[6][...]).astype(BF)

    def shard(total, own, i, o):
        d_branch, dg0 = rms_back(i[2][own].astype(F32), i[17][0, 0:1], total)
        o[1][...] = dg0
        dx16 = (i[1][...] + d_branch).astype(BF)
        if below is None:
            return [dx16]
        d_mlp, dg3 = rms_back(i[19][...], i[20][0, 3:4], dx16.astype(F32))
        o[7][...] = dg3
        return [dx16, d_mlp.astype(BF)]

    ins = [d_att16, dr, x16, n1, qr, kr, q, k, v, p, mix, cos, sin]
    ins += [w_query, w_key, w_value, w_out, norm_gains, head_gains]
    outs = [
        struct((width, 4 * hd), BF),
        struct((1, width)),
        struct((1, hd)),
        struct((1, hd)),
        struct((rows, hd), BF),
        struct((rows, hd), BF),
        struct((rows, hd), BF),
    ]
    if below is not None:
        ins += list(below)
        outs.append(struct((1, width)))
    return call_exchange(ins, outs, 1 if below is None else 2, pre, during, shard, ranks, cid, behind)


def reduce_kernel(job, nt, nd, hd, *refs):
    (ga0, ra1, rm0, rm1, s0, s1, y0, y1, x0, x1) = refs[:10]
    (out_a, out_m, out_kv, out_s, out_y, out_x) = refs[10:16]
    (swap_s, ra0, both_a, kv_part, kv_recv, s_sum, s_recv) = refs[16:23]
    (sm_send, sm_recv, lo_sem, kt_send, kt_recv, ka_send, ka_recv, ss_send, ss_recv) = refs[23:32]
    sec = lax.axis_index("section")
    t = lax.axis_index("tensor")
    z = lax.axis_index("dp")
    total = nt * nd
    me = z * nt + t
    section = {"section": 1 - sec}
    group = []
    for step in range(1, total):
        flat = lax.rem(me + step, total)
        group.append({"dp": flat // nt, "tensor": lax.rem(flat, nt)})
    barrier = pltpu.get_barrier_semaphore()
    for device in [section] + group:
        pl.semaphore_signal(barrier, inc=1, device_id=device, device_id_type=MESH)
    pl.semaphore_wait(barrier, total)

    def remote(src, dst, send, recv, device):
        return pltpu.make_async_remote_copy(
            src_ref=src, dst_ref=dst, send_sem=send, recv_sem=recv,
            device_id=device, device_id_type=MESH,
        )

    mine_rows = pl.ds(pl.multiple_of(sec * job.half, job.half), job.half)

    def swap(s, m, y, x):
        return [
            remote(s, swap_s, sm_send.at[0], sm_recv.at[0], section),
            remote(m, out_m.at[mine_rows], sm_send.at[1], sm_recv.at[1], section),
            remote(y, out_y.at[sec], sm_send.at[2], sm_recv.at[2], section),
            remote(x, out_x.at[sec], sm_send.at[3], sm_recv.at[3], section),
        ]

    def keep(m, y, x):
        return [
            pltpu.make_async_copy(m, out_m.at[mine_rows], lo_sem.at[0]),
            pltpu.make_async_copy(y, out_y.at[sec], lo_sem.at[1]),
            pltpu.make_async_copy(x, out_x.at[sec], lo_sem.at[2]),
        ]

    job.begin(ga0, refs[32:])

    @pl.when(sec == 0)
    def _():
        for copy in swap(s1, rm1, y1, x1) + keep(rm0, y0, x0):
            copy.start()

    @pl.when(sec == 1)
    def _():
        for copy in swap(s0, rm0, y0, x0) + keep(rm1, y1, x1):
            copy.start()

    job.send()
    waits = swap(s0, rm0, y0, x0)
    waits[0].wait_recv()

    @pl.when(sec == 0)
    def _():
        s_sum[...] = s0[...] + swap_s[...]

    @pl.when(sec == 1)
    def _():
        s_sum[...] = s1[...] + swap_s[...]

    s_copies = []
    for step, device in enumerate(group):
        copy = remote(s_sum, s_recv.at[step], ss_send.at[step], ss_recv.at[step], device)
        copy.start()
        s_copies.append(copy)
    ra0[...] = job.finish()

    def swap_a(a):
        return remote(a, both_a.at[mine_rows], sm_send.at[4], sm_recv.at[4], section)

    @pl.when(sec == 0)
    def _():
        swap_a(ra1).start()
        both_a[mine_rows] = ra0[...]

    @pl.when(sec == 1)
    def _():
        swap_a(ra0).start()
        both_a[mine_rows] = ra1[...]

    waits.append(swap_a(ra0))
    waits[4].wait_recv()
    out_a[...] = both_a[:, : 2 * hd]
    piece = 2 * hd // nt
    for n in range(nt):
        kv_part[n] = both_a[:, 2 * hd + n * piece : 2 * hd + (n + 1) * piece].astype(BF)
    kt_copies = []
    for d in range(1, nt):
        peer = lax.rem(t + d, nt)
        copy = remote(
            kv_part.at[peer], kv_recv.at[d - 1], kt_send.at[d - 1], kt_recv.at[d - 1], {"tensor": peer}
        )
        copy.start()
        kt_copies.append(copy)
    mine = kv_part[t].astype(F32)
    for d, copy in enumerate(kt_copies):
        copy.wait_recv()
        mine = mine + kv_recv[d].astype(F32)
    out_kv[me] = mine.astype(BF)
    ka_copies = []
    for step, device in enumerate(group):
        copy = remote(out_kv.at[me], out_kv.at[me], ka_send.at[step], ka_recv.at[step], device)
        copy.start()
        ka_copies.append(copy)
    acc_s = s_sum[...]
    for step, copy in enumerate(s_copies):
        copy.wait_recv()
        acc_s = acc_s + s_recv[step]
    out_s[...] = acc_s
    for copy in waits[1:4]:
        copy.wait_recv()
    for copy in keep(rm0, y0, x0):
        copy.wait()
    for copy in ka_copies:
        copy.wait()
    for copy in waits + s_copies + kt_copies:
        copy.wait_send()


def reduce_all(grads_a, grads_m, smalls, ys, xs, nt, nd, hd):
    job = GradSum(nd, grads_a[0])
    wa, wm = grads_a[0].shape[1], grads_m[0].shape[1]
    rows = 2 * job.half
    total = nt * nd
    dma = pltpu.SemaphoreType.DMA
    ins = list(grads_a) + list(grads_m) + list(smalls) + list(ys) + list(xs)
    tok = ys[0].shape
    return pl.pallas_call(
        functools.partial(reduce_kernel, job, nt, nd, hd),
        out_shape=[
            struct((rows, 2 * hd)),
            struct((rows, wm)),
            struct((total, rows, 2 * hd // nt), BF),
            struct(smalls[0].shape),
            struct((2,) + tok, BF),
            struct((2,) + tok, BF),
        ],
        in_specs=[VM] * len(ins),
        out_specs=[VM] * 6,
        scratch_shapes=[
            pltpu.VMEM(smalls[0].shape, F32),
            pltpu.VMEM((job.half, wa), F32),
            pltpu.VMEM((rows, wa), F32),
            pltpu.VMEM((nt, rows, 2 * hd // nt), BF),
            pltpu.VMEM((nt - 1, rows, 2 * hd // nt), BF),
            pltpu.VMEM(smalls[0].shape, F32),
            pltpu.VMEM((total - 1,) + smalls[0].shape, F32),
            dma((5,)), dma((5,)), dma((3,)), dma((nt - 1,)), dma((nt - 1,)),
            dma((total - 1,)), dma((total - 1,)), dma((total - 1,)), dma((total - 1,)),
        ]
        + job.scratch(),
        compiler_params=pltpu.CompilerParams(
            collective_id=2, has_side_effects=True, vmem_limit_bytes=VMEM_LIMIT
        ),
    )(*ins)


def reduce_plain(grads_a, grads_m, smalls, ys, xs, nt, nd, hd):
    sec = lax.axis_index("section")
    pairs = [(0, 1), (1, 0)]

    def own_sum(pair):
        own = jnp.where(sec == 0, pair[0], pair[1])
        other = jnp.where(sec == 0, pair[1], pair[0])
        return own.astype(F32) + lax.ppermute(other, "section", pairs).astype(F32)

    def placed(pair):
        own = jnp.where(sec == 0, pair[0], pair[1])
        other = lax.ppermute(jnp.where(sec == 0, pair[1], pair[0]), "section", pairs)
        return jnp.stack([jnp.where(sec == 0, own, other), jnp.where(sec == 0, other, own)])

    g_a, g_m, small = own_sum(grads_a), own_sum(grads_m), own_sum(smalls)
    split = jnp.concatenate([g_a[:, : 2 * hd], g_m], axis=1).astype(BF)
    split = lax.psum_scatter(split, "dp", scatter_dimension=0, tiled=True).astype(F32)
    kv, small = lax.psum((g_a[:, 2 * hd :], small), ("tensor", "dp"))
    return split[:, : 2 * hd], split[:, 2 * hd :], kv, small, placed(ys), placed(xs)


def per_device(tokens, segments, cotangent, *weights):
    nt, nd = lax.axis_size("tensor"), lax.axis_size("dp")
    sec = lax.axis_index("section")
    width = tokens.shape[1]
    hd = weights[1].shape[-1]
    units = weights[4].shape[-1]
    rows = MB_TOK
    x16 = lax.dynamic_slice_in_dim(tokens, sec * rows, rows, 0)
    cot = lax.dynamic_slice_in_dim(cotangent, sec * rows, rows, 0)
    seg = lax.dynamic_slice_in_dim(segments, sec * rows, rows, 0)
    w0, w1 = both_layers(weights)
    at = jnp.arange(rows, dtype=jnp.int32)
    seen = (seg[:, None] == seg[None, :]) & (at[None, :] <= at[:, None])
    position = (jnp.sum(seen.astype(jnp.int32), axis=1) - 1).astype(F32)
    freq = jnp.exp(jnp.arange(hd // 2, dtype=F32) * (-2.0 * math.log(10000.0) / hd))
    angles = position[:, None] * freq[None, :]
    tables = (jnp.cos(angles), jnp.sin(angles), seg[:, None], seg[None, :])

    n2_0, *kept_0, att_0, res_0 = attend_forward(x16, w0, tables, nt, 3)
    y_0, gate_0, up_0, h_0, mlp_0 = feed_forward(n2_0, res_0, w0, None, nt, 4)
    n2_1, *kept_1, att_1, res_1 = attend_forward(y_0, w1, tables, nt, 3)
    y_1, d_mlp_1, gate_1, up_1, h_1, _, dg3_1 = feed_forward(n2_1, res_1, w1, cot, nt, 5)

    d_att_1, gm_1, dr_1, dg1_1, dg2_1, _, _ = feed_backward(
        d_mlp_1, cot, (n2_1, gate_1, up_1, h_1, res_1, att_1), w1, nt, 6
    )
    fits = width % (32 * nd) == 0 and (2 * hd // nt) % 128 == 0 and nt * nd <= 32
    dx_1, d_mlp_0, ga_1, dg0_1, dgq_1, dgk_1, _, _, _, dg3_0, *sum_m1 = attend_backward(
        d_att_1, dr_1, y_0, kept_1, w1, tables, (mlp_0, w0[7]), nt, 7, gm_1 if fits else None
    )
    d_att_0, gm_0, dr_0, dg1_0, dg2_0, _, _, *sum_a1 = feed_backward(
        d_mlp_0, dx_1, (n2_0, gate_0, up_0, h_0, res_0, att_0), w0, nt, 9, ga_1 if fits else None
    )
    dx_0, ga_0, dg0_0, dgq_0, dgk_0, _, _, _, *sum_m0 = attend_backward(
        d_att_0, dr_0, x16, kept_0, w0, tables, None, nt, 8, gm_0 if fits else None
    )
    if fits:
        ga_1, gm_0, gm_1 = sum_a1[0], sum_m0[0], sum_m1[0]

    def small(g0, g1, g2, g3, q, k):
        tail = ((0, 2), (0, width - hd))
        return jnp.concatenate([g0, g1, g2, g3, jnp.pad(jnp.concatenate([q, k]), tail)])

    smalls = (
        small(dg0_0, dg1_0, dg2_0, dg3_0, dgq_0, dgk_0),
        small(dg0_1, dg1_1, dg2_1, dg3_1, dgq_1, dgk_1),
    )
    reducer = reduce_all if fits else reduce_plain
    g_a, g_m, kv, sums, out_y, out_x = reducer(
        (ga_0, ga_1), (gm_0, gm_1), smalls, (y_0, y_1), (dx_0, dx_1), nt, nd, hd
    )
    if fits:
        kv = kv.reshape(nd, nt, width // nd, 2 * hd // nt).transpose(0, 2, 1, 3).reshape(width, 2 * hd)
        kv = kv.astype(F32)
    cols = width // nd
    gains = lax.dynamic_slice(sums, (0, lax.axis_index("dp") * cols), (4, cols))
    return (
        out_y.astype(F32).reshape(1, 2 * rows, width),
        out_x.astype(F32).reshape(1, 2 * rows, width),
        g_a[None, :, :hd],
        kv[None, :, :hd],
        kv[None, :, hd:],
        g_a[:, hd:].T[None],
        g_m[None, :, :units],
        g_m[None, :, units : 2 * units],
        g_m[:, 2 * units :].T[None],
        gains[None],
        sums[None, 4:6, :hd],
    )


def solution(mesh):
    return jax.shard_map(
        per_device,
        mesh=mesh,
        in_specs=(
            P("dp", None),
            P("dp"),
            P("dp", None),
            P("section", None, "tensor"),
            P("section", None, None),
            P("section", None, None),
            P("section", "tensor", None),
            P("section", None, "tensor"),
            P("section", None, "tensor"),
            P("section", "tensor", None),
            P("section", None, None),
            P("section", None, None),
        ),
        out_specs=(
            P("section", "dp", None),
            P("section", "dp", None),
            P("section", "dp", "tensor"),
            P("section", None, None),
            P("section", None, None),
            P("section", "tensor", "dp"),
            P("section", "dp", "tensor"),
            P("section", "dp", "tensor"),
            P("section", "tensor", "dp"),
            P("section", None, "dp"),
            P("section", None, None),
        ),
        check_vma=False,
    )
```

```python
import functools
import math

import jax
import jax.numpy as jnp
from jax import lax
from jax.experimental import pallas as pl
from jax.experimental.pallas import tpu as pltpu
from jax.sharding import PartitionSpec as P

WINDOW = 512
MB_TOK = 256
EPSILON = 1e-06
BF = jnp.bfloat16
F32 = jnp.float32
MESH = pl.DeviceIdType.MESH
VM = pl.BlockSpec(memory_space=pltpu.VMEM)
VMEM_LIMIT = 50 * 1024 * 1024


def mm(a, b):
    return lax.dot_general(a, b, (((1,), (0,)), ((), ())), preferred_element_type=F32)


def mm_t(a, b):
    return lax.dot_general(a, b, (((1,), (1,)), ((), ())), preferred_element_type=F32)


def t_mm(a, b):
    return lax.dot_general(a, b, (((0,), (0,)), ((), ())), preferred_element_type=F32)


def inverse_rms(v):
    return lax.rsqrt(jnp.mean(v * v, axis=-1, keepdims=True) + EPSILON)


def rms(v):
    return v * inverse_rms(v)


def rms_back(v, gain, cot):
    inv = inverse_rms(v)
    unit = v * inv
    weighted = cot * gain
    d_v = inv * (weighted - unit * jnp.mean(weighted * unit, axis=-1, keepdims=True))
    return d_v, jnp.sum(cot * unit, axis=0, keepdims=True)


def rope(u, cos, sin):
    half = u.shape[-1] // 2
    a, b = u[:, :half], u[:, half:]
    return jnp.concatenate([a * cos - b * sin, b * cos + a * sin], axis=-1)


def rope_back(d, cos, sin):
    half = d.shape[-1] // 2
    a, b = d[:, :half], d[:, half:]
    return jnp.concatenate([a * cos + b * sin, b * cos - a * sin], axis=-1)


GELU_C = math.sqrt(2.0 / math.pi)


def gelu_parts(g):
    th = jnp.tanh(GELU_C * (g + 0.044715 * g * g * g))
    value = 0.5 * g * (1.0 + th)
    slope = 0.5 * (1.0 + th) + 0.5 * g * (1.0 - th * th) * GELU_C * (1.0 + 3 * 0.044715 * g * g)
    return value, slope


class GradSum:
    def __init__(self, nd, grad):
        self.nd = nd
        self.half = grad.shape[0] // (2 * nd)
        self.width = grad.shape[1]

    def scratch(self):
        dma = pltpu.SemaphoreType.DMA
        block = (self.half, self.width)
        return [
            pltpu.VMEM((self.nd,) + block, BF),
            pltpu.VMEM((self.nd,) + block, BF),
            pltpu.VMEM((self.nd - 1,) + block, BF),
            dma((self.nd,)), dma((self.nd,)), dma((self.nd - 1,)), dma((self.nd - 1,)),
        ]

    def result(self):
        return struct((self.half, self.width))

    def devices(self):
        z = lax.axis_index("dp")
        peers = [{"dp": lax.rem(z + d, self.nd)} for d in range(1, self.nd)]
        return [{"section": 1 - lax.axis_index("section")}] + peers

    def begin(self, grad, refs):
        self.grad = grad
        self.got, self.held, self.landed, sw_send, sw_recv, self.dp_send, self.dp_recv = refs
        sec, z = lax.axis_index("section"), lax.axis_index("dp")
        self.zs = [lax.rem(z + d, self.nd) for d in range(1, self.nd)] + [z]
        self.swaps = []
        for n, peer in enumerate(self.zs):
            copy = pltpu.make_async_remote_copy(
                src_ref=grad.at[self.rows(peer, 1 - sec)],
                dst_ref=self.got.at[n],
                send_sem=sw_send.at[n],
                recv_sem=sw_recv.at[n],
                device_id={"section": 1 - sec},
                device_id_type=MESH,
            )
            copy.start()
            self.swaps.append(copy)

    def rows(self, peer, core):
        return pl.ds(pl.multiple_of((2 * peer + core) * self.half, self.half), self.half)

    def send(self):
        sec = lax.axis_index("section")
        self.sends = []
        for n, peer in enumerate(self.zs):
            self.swaps[n].wait_recv()
            own = self.grad[self.rows(peer, sec)].astype(F32)
            self.held[n] = (own + self.got[n].astype(F32)).astype(BF)
            if n < self.nd - 1:
                copy = pltpu.make_async_remote_copy(
                    src_ref=self.held.at[n],
                    dst_ref=self.landed.at[n],
                    send_sem=self.dp_send.at[n],
                    recv_sem=self.dp_recv.at[n],
                    device_id={"dp": peer},
                    device_id_type=MESH,
                )
                copy.start()
                self.sends.append(copy)

    def finish(self):
        total = self.held[self.nd - 1].astype(F32)
        for n, copy in enumerate(self.sends):
            copy.wait_recv()
            total = total + self.landed[n].astype(F32)
        for copy in self.swaps + self.sends:
            copy.wait_send()
        return total


def call_exchange(ins, out_shapes, gathered, pre, during, shard, ranks, collective_id, behind=None):
    job = None
    if behind is not None:
        job = GradSum(lax.axis_size("dp"), behind)
        ins = ins + [behind]
        out_shapes = out_shapes + [job.result()]
    n_in, n_out = len(ins), len(out_shapes)
    rows, width = MB_TOK, ins[0].shape[-1]
    share = rows // ranks

    def kernel(*refs):
        in_refs = refs[:n_in]
        gat = refs[n_in : n_in + gathered]
        outs = refs[n_in + gathered : n_in + gathered + n_out]
        scratch = refs[n_in + gathered + n_out :]
        part, recv, rs_send, rs_recv, ag_send, ag_recv = scratch[:6]
        me = lax.axis_index("tensor")
        peers = [lax.rem(me + d, ranks) for d in range(1, ranks)]
        barrier = pltpu.get_barrier_semaphore()
        devices = [{"tensor": peer} for peer in peers] + (job.devices() if job else [])
        for device in devices:
            pl.semaphore_signal(barrier, inc=1, device_id=device, device_id_type=MESH)
        own = pl.ds(pl.multiple_of(me * share, share), share)
        if job:
            pl.semaphore_wait(barrier, len(devices))
            job.begin(in_refs[-1], scratch[6:])
        part[...] = pre(in_refs, outs).astype(BF)
        if not job:
            pl.semaphore_wait(barrier, len(devices))
        copies = []
        for d, peer in enumerate(peers):
            copy = pltpu.make_async_remote_copy(
                src_ref=part.at[pl.ds(pl.multiple_of(peer * share, share), share)],
                dst_ref=recv.at[d],
                send_sem=rs_send.at[d],
                recv_sem=rs_recv.at[d],
                device_id={"tensor": peer},
                device_id_type=MESH,
            )
            copy.start()
            copies.append(copy)
        if job:
            job.send()
        if during is not None:
            during(in_refs, outs)
        total = part[own].astype(F32)
        for d, copy in enumerate(copies):
            copy.wait_recv()
            total = total + recv[d].astype(F32)
        results = shard(total, own, in_refs, outs)
        sends = []
        for i in range(gathered):
            gat[i][own] = results[i]
            for d, peer in enumerate(peers):
                copy = pltpu.make_async_remote_copy(
                    src_ref=gat[i].at[own],
                    dst_ref=gat[i].at[own],
                    send_sem=ag_send.at[i, d],
                    recv_sem=ag_recv.at[i, d],
                    device_id={"tensor": peer},
                    device_id_type=MESH,
                )
                copy.start()
                sends.append(copy)
        for copy in copies:
            copy.wait_send()
        for copy in sends:
            copy.wait()
        if job:
            outs[-1][...] = job.finish()

    return pl.pallas_call(
        kernel,
        out_shape=[jax.ShapeDtypeStruct((rows, width), BF)] * gathered + out_shapes,
        in_specs=[VM] * n_in,
        out_specs=[VM] * (gathered + n_out),
        scratch_shapes=[
            pltpu.VMEM((rows, width), BF),
            pltpu.VMEM((ranks - 1, share, width), BF),
            pltpu.SemaphoreType.DMA((ranks - 1,)),
            pltpu.SemaphoreType.DMA((ranks - 1,)),
            pltpu.SemaphoreType.DMA((gathered, ranks - 1)),
            pltpu.SemaphoreType.DMA((gathered, ranks - 1)),
        ]
        + (job.scratch() if job else []),
        compiler_params=pltpu.CompilerParams(
            collective_id=collective_id, has_side_effects=True, vmem_limit_bytes=VMEM_LIMIT
        ),
    )(*ins)


def swap_kernel(count, *refs):
    ins, firsts, seconds = refs[:count], refs[count : 2 * count], refs[2 * count : 3 * count]
    local_sem, send_sem, recv_sem = refs[3 * count :]
    me = lax.axis_index("section")
    other = 1 - me
    barrier = pltpu.get_barrier_semaphore()
    pl.semaphore_signal(barrier, inc=1, device_id={"section": other}, device_id_type=MESH)
    pl.semaphore_wait(barrier, 1)
    for sec, outs in ((0, firsts), (1, seconds)):

        @pl.when(me == sec)
        def _():
            copies = []
            for i in range(count):
                far = pltpu.make_async_remote_copy(
                    src_ref=ins[i],
                    dst_ref=outs[i],
                    send_sem=send_sem.at[i],
                    recv_sem=recv_sem.at[i],
                    device_id={"section": other},
                    device_id_type=MESH,
                )
                near = pltpu.make_async_copy(ins[i], outs[i], local_sem.at[i])
                far.start()
                near.start()
                copies += [far, near]
            for copy in copies:
                copy.wait()


def both_layers(weights):
    count = len(weights)
    shapes = [jax.ShapeDtypeStruct(w.shape, w.dtype) for w in weights]
    outs = pl.pallas_call(
        functools.partial(swap_kernel, count),
        out_shape=shapes * 2,
        in_specs=[VM] * count,
        out_specs=[VM] * (2 * count),
        scratch_shapes=[pltpu.SemaphoreType.DMA((count,))] * 3,
        compiler_params=pltpu.CompilerParams(
            collective_id=1, has_side_effects=True, vmem_limit_bytes=VMEM_LIMIT
        ),
    )(*weights)
    return outs[:count], outs[count:]


def struct(shape, dtype=F32):
    return jax.ShapeDtypeStruct(shape, dtype)


def attend_forward(x16, w, tables, ranks, cid):
    w_query, w_key, w_value, w_out, _, _, _, norm_gains, head_gains = w
    cos, sin, seg_col, seg_row = tables
    width = x16.shape[1]
    hd = w_key.shape[-1]
    rows = MB_TOK

    def pre(i, o):
        x_ref, wq, wk, wv, wo, ng, hg, cos, sin, sc, sr = i
        n1_o, qr_o, kr_o, q_o, k_o, v_o, p_o, mix_o = o[:8]
        n1 = (rms(x_ref[...].astype(F32)) * ng[0, 0:1]).astype(BF)
        n1_o[...] = n1
        qr = mm(n1, wq[0])
        kr = mm(n1, wk[0])
        v = mm(n1, wv[0]).astype(BF)
        qr_o[...] = qr
        kr_o[...] = kr
        v_o[...] = v
        q = rope(rms(qr) * hg[0, 0:1], cos[...], sin[...]).astype(BF)
        k = rope(rms(kr) * hg[0, 1:2], cos[...], sin[...]).astype(BF)
        q_o[...] = q
        k_o[...] = k
        at = lax.broadcasted_iota(jnp.int32, (rows, rows), 0)
        to = lax.broadcasted_iota(jnp.int32, (rows, rows), 1)
        allowed = (sc[...] == sr[...]) & (to <= at) & (at - to < WINDOW)
        s = jnp.where(allowed, mm_t(q, k) * (hd**-0.5), -1e30)
        e = jnp.exp(s - jnp.max(s, axis=-1, keepdims=True))
        p = e / jnp.sum(e, axis=-1, keepdims=True)
        p_o[...] = p
        mix = mm(p.astype(BF), v).astype(BF)
        mix_o[...] = mix
        return mm(mix, wo[0])

    def shard(total, own, i, o):
        ng = i[5]
        residual = i[0][own].astype(F32) + rms(total) * ng[0, 1:2]
        o[8][...] = total
        o[9][...] = residual
        return [(rms(residual) * ng[0, 2:3]).astype(BF)]

    share = rows // ranks
    return call_exchange(
        [x16, w_query, w_key, w_value, w_out, norm_gains, head_gains, cos, sin, seg_col, seg_row],
        [
            struct((rows, width), BF),
            struct((rows, hd)),
            struct((rows, hd)),
            struct((rows, hd), BF),
            struct((rows, hd), BF),
            struct((rows, hd), BF),
            struct((rows, rows)),
            struct((rows, hd), BF),
            struct((share, width)),
            struct((share, width)),
        ],
        1, pre, None, shard, ranks, cid,
    )


def feed_forward(n2, residual, w, cot, ranks, cid):
    _, _, _, _, w_gate, w_up, w_down, norm_gains, _ = w
    width = n2.shape[1]
    units = w_gate.shape[-1]
    rows = MB_TOK
    share = rows // ranks

    def pre(i, o):
        n2_ref, res, wg, wu, wd, ng = i[:6]
        n2 = n2_ref[...]
        gate = mm(n2, wg[0])
        up = mm(n2, wu[0])
        h = (gelu_parts(gate)[0] * up).astype(BF)
        o[0][...] = gate
        o[1][...] = up
        o[2][...] = h
        return mm(h, wd[0])

    def shard(total, own, i, o):
        res, ng = i[1], i[5]
        gain = ng[0, 3:4]
        y16 = (res[...] + rms(total) * gain).astype(BF)
        o[3][...] = total
        if cot is None:
            return [y16]
        d_mlp, d_gain = rms_back(total, gain, i[6][own].astype(F32))
        o[4][...] = d_gain
        return [y16, d_mlp.astype(BF)]

    outs = [struct((rows, units)), struct((rows, units)), struct((rows, units), BF), struct((share, width))]
    ins = [n2, residual, w_gate, w_up, w_down, norm_gains]
    if cot is not None:
        ins.append(cot)
        outs.append(struct((1, width)))
    return call_exchange(ins, outs, 1 if cot is None else 2, pre, None, shard, ranks, cid)


def feed_backward(d_mlp16, dy16, kept, w, ranks, cid, behind=None):
    _, _, _, _, w_gate, w_up, w_down, norm_gains, _ = w
    n2, gate, up, h, residual, attended = kept
    width = n2.shape[1]
    units = w_gate.shape[-1]
    rows = MB_TOK
    share = rows // ranks

    def pre(i, o):
        dm, _, _, gate, up, _, _, _, wg, wu, wd, _ = i[:12]
        dh = mm_t(dm[...], wd[0])
        value, slope = gelu_parts(gate[...])
        dg = (dh * up[...] * slope).astype(BF)
        du = (dh * value).astype(BF)
        o[4][...] = dg
        o[5][...] = du
        return mm_t(dg, wg[0]) + mm_t(du, wu[0])

    def during(i, o):
        dm, n2, h = i[0], i[2], i[5]
        o[0][:, :units] = t_mm(n2[...], o[4][...]).astype(BF)
        o[0][:, units : 2 * units] = t_mm(n2[...], o[5][...]).astype(BF)
        o[0][:, 2 * units :] = t_mm(dm[...], h[...]).astype(BF)

    def shard(total, own, i, o):
        dy, res, att, ng = i[1], i[6], i[7], i[11]
        d_branch, dg2 = rms_back(res[...], ng[0, 2:3], total)
        dr = dy[own].astype(F32) + d_branch
        d_att, dg1 = rms_back(att[...], ng[0, 1:2], dr)
        o[1][...] = dr
        o[2][...] = dg1
        o[3][...] = dg2
        return [d_att.astype(BF)]

    return call_exchange(
        [d_mlp16, dy16, n2, gate, up, h, residual, attended, w_gate, w_up, w_down, norm_gains],
        [
            struct((width, 3 * units), BF),
            struct((share, width)),
            struct((1, width)),
            struct((1, width)),
            struct((rows, units), BF),
            struct((rows, units), BF),
        ],
        1, pre, during, shard, ranks, cid, behind,
    )


def attend_backward(d_att16, dr, x16, kept, w, tables, below, ranks, cid, behind=None):
    w_query, w_key, w_value, w_out, _, _, _, norm_gains, head_gains = w
    n1, qr, kr, q, k, v, p, mix = kept
    cos, sin = tables[:2]
    width = n1.shape[1]
    hd = w_key.shape[-1]
    rows = MB_TOK

    def pre(i, o):
        da, _, _, n1, qr, kr, q, k, v, p, mix, cos, sin, wq, wk, wv, wo, _, hg = i[:19]
        scale = hd**-0.5
        do = mm_t(da[...], wo[0]).astype(BF)
        p = p[...]
        d_p = mm_t(do, v[...])
        ds = (p * (d_p - jnp.sum(p * d_p, axis=-1, keepdims=True))).astype(BF)
        dq = mm(ds, k[...]) * scale
        dk = t_mm(ds, q[...]) * scale
        dv = t_mm(p.astype(BF), do).astype(BF)
        dq_raw, dgq = rms_back(qr[...], hg[0, 0:1], rope_back(dq, cos[...], sin[...]))
        dk_raw, dgk = rms_back(kr[...], hg[0, 1:2], rope_back(dk, cos[...], sin[...]))
        dq_raw = dq_raw.astype(BF)
        dk_raw = dk_raw.astype(BF)
        o[2][...] = dgq
        o[3][...] = dgk
        o[4][...] = dq_raw
        o[5][...] = dk_raw
        o[6][...] = dv
        return mm_t(dq_raw, wq[0]) + mm_t(dk_raw, wk[0]) + mm_t(dv, wv[0])

    def during(i, o):
        da, n1, mix = i[0][...], i[3][...], i[10][...]
        o[0][:, :hd] = t_mm(n1, o[4][...]).astype(BF)
        o[0][:, hd : 2 * hd] = t_mm(da, mix).astype(BF)
        o[0][:, 2 * hd : 3 * hd] = t_mm(n1, o[5][...]).astype(BF)
        o[0][:, 3 * hd :] = t_mm(n1, o[6][...]).astype(BF)

    def shard(total, own, i, o):
        d_branch, dg0 = rms_back(i[2][own].astype(F32), i[17][0, 0:1], total)
        o[1][...] = dg0
        dx16 = (i[1][...] + d_branch).astype(BF)
        if below is None:
            return [dx16]
        d_mlp, dg3 = rms_back(i[19][...], i[20][0, 3:4], dx16.astype(F32))
        o[7][...] = dg3
        return [dx16, d_mlp.astype(BF)]

    ins = [d_att16, dr, x16, n1, qr, kr, q, k, v, p, mix, cos, sin]
    ins += [w_query, w_key, w_value, w_out, norm_gains, head_gains]
    outs = [
        struct((width, 4 * hd), BF),
        struct((1, width)),
        struct((1, hd)),
        struct((1, hd)),
        struct((rows, hd), BF),
        struct((rows, hd), BF),
        struct((rows, hd), BF),
    ]
    if below is not None:
        ins += list(below)
        outs.append(struct((1, width)))
    return call_exchange(ins, outs, 1 if below is None else 2, pre, during, shard, ranks, cid, behind)


def reduce_kernel(job, nt, nd, hd, *refs):
    (ga0, ra1, rm0, rm1, s0, s1, y0, y1, x0, x1) = refs[:10]
    (out_a, out_m, out_kv, out_s, out_y, out_x) = refs[10:16]
    (swap_s, ra0, both_a, kv_part, kv_recv, s_sum, s_recv) = refs[16:23]
    (sm_send, sm_recv, lo_sem, kt_send, kt_recv, ka_send, ka_recv, ss_send, ss_recv) = refs[23:32]
    sec = lax.axis_index("section")
    t = lax.axis_index("tensor")
    z = lax.axis_index("dp")
    total = nt * nd
    me = z * nt + t
    section = {"section": 1 - sec}
    across = [{"dp": lax.rem(z + d, nd)} for d in range(1, nd)]
    within = [{"tensor": lax.rem(t + d, nt)} for d in range(1, nt)]
    group = across + within
    barrier = pltpu.get_barrier_semaphore()
    for device in [section] + group:
        pl.semaphore_signal(barrier, inc=1, device_id=device, device_id_type=MESH)
    pl.semaphore_wait(barrier, 1 + len(group))

    def remote(src, dst, send, recv, device):
        return pltpu.make_async_remote_copy(
            src_ref=src, dst_ref=dst, send_sem=send, recv_sem=recv,
            device_id=device, device_id_type=MESH,
        )

    mine_rows = pl.ds(pl.multiple_of(sec * job.half, job.half), job.half)

    def swap(s, m, y, x):
        return [
            remote(s, swap_s, sm_send.at[0], sm_recv.at[0], section),
            remote(m, out_m.at[mine_rows], sm_send.at[1], sm_recv.at[1], section),
            remote(y, out_y.at[sec], sm_send.at[2], sm_recv.at[2], section),
            remote(x, out_x.at[sec], sm_send.at[3], sm_recv.at[3], section),
        ]

    def keep(m, y, x):
        return [
            pltpu.make_async_copy(m, out_m.at[mine_rows], lo_sem.at[0]),
            pltpu.make_async_copy(y, out_y.at[sec], lo_sem.at[1]),
            pltpu.make_async_copy(x, out_x.at[sec], lo_sem.at[2]),
        ]

    job.begin(ga0, refs[32:])

    @pl.when(sec == 0)
    def _():
        for copy in swap(s1, rm1, y1, x1) + keep(rm0, y0, x0):
            copy.start()

    @pl.when(sec == 1)
    def _():
        for copy in swap(s0, rm0, y0, x0) + keep(rm1, y1, x1):
            copy.start()

    job.send()
    waits = swap(s0, rm0, y0, x0)
    waits[0].wait_recv()

    @pl.when(sec == 0)
    def _():
        s_sum[...] = s0[...] + swap_s[...]

    @pl.when(sec == 1)
    def _():
        s_sum[...] = s1[...] + swap_s[...]

    s_copies = []
    for step, device in enumerate(across):
        copy = remote(s_sum, s_recv.at[step], ss_send.at[step], ss_recv.at[step], device)
        copy.start()
        s_copies.append(copy)
    ra0[...] = job.finish()

    def swap_a(a):
        return remote(a, both_a.at[mine_rows], sm_send.at[4], sm_recv.at[4], section)

    @pl.when(sec == 0)
    def _():
        swap_a(ra1).start()
        both_a[mine_rows] = ra0[...]

    @pl.when(sec == 1)
    def _():
        swap_a(ra0).start()
        both_a[mine_rows] = ra1[...]

    waits.append(swap_a(ra0))
    waits[4].wait_recv()
    out_a[...] = both_a[:, : 2 * hd]
    piece = 2 * hd // nt
    for n in range(nt):
        kv_part[n] = both_a[:, 2 * hd + n * piece : 2 * hd + (n + 1) * piece].astype(BF)
    kt_copies = []
    for d in range(1, nt):
        peer = lax.rem(t + d, nt)
        copy = remote(
            kv_part.at[peer], kv_recv.at[d - 1], kt_send.at[d - 1], kt_recv.at[d - 1], {"tensor": peer}
        )
        copy.start()
        kt_copies.append(copy)
    mine = kv_part[t].astype(F32)
    for d, copy in enumerate(kt_copies):
        copy.wait_recv()
        mine = mine + kv_recv[d].astype(F32)
    out_kv[me] = mine.astype(BF)
    ka_copies = []
    for step, device in enumerate(across):
        copy = remote(out_kv.at[me], out_kv.at[me], ka_send.at[step], ka_recv.at[step], device)
        copy.start()
        ka_copies.append(copy)
    acc_s = s_sum[...]
    for step, copy in enumerate(s_copies):
        copy.wait_recv()
        acc_s = acc_s + s_recv[step]
    out_s[...] = acc_s
    late = []
    for d, device in enumerate(within):
        step = nd - 1 + d
        copy = remote(out_s, s_recv.at[step], ss_send.at[step], ss_recv.at[step], device)
        copy.start()
        late.append(copy)
    step = nd - 1
    for back in range(nd):
        row = lax.rem(z + nd - back, nd) * nt + t
        if back > 0:
            ka_copies[back - 1].wait_recv()
        for device in within:
            copy = remote(out_kv.at[row], out_kv.at[row], ka_send.at[step], ka_recv.at[step], device)
            copy.start()
            late.append(copy)
            step += 1
    for d in range(nt - 1):
        late[d].wait()
        acc_s = acc_s + s_recv[nd - 1 + d]
    out_s[...] = acc_s
    for copy in waits[1:4]:
        copy.wait_recv()
    for copy in keep(rm0, y0, x0):
        copy.wait()
    for copy in late[nt - 1 :]:
        copy.wait()
    for copy in waits + s_copies + kt_copies + ka_copies:
        copy.wait_send()


def reduce_all(grads_a, grads_m, smalls, ys, xs, nt, nd, hd):
    job = GradSum(nd, grads_a[0])
    wa, wm = grads_a[0].shape[1], grads_m[0].shape[1]
    rows = 2 * job.half
    total = nt * nd
    dma = pltpu.SemaphoreType.DMA
    ins = list(grads_a) + list(grads_m) + list(smalls) + list(ys) + list(xs)
    tok = ys[0].shape
    return pl.pallas_call(
        functools.partial(reduce_kernel, job, nt, nd, hd),
        out_shape=[
            struct((rows, 2 * hd)),
            struct((rows, wm)),
            struct((total, rows, 2 * hd // nt), BF),
            struct(smalls[0].shape),
            struct((2,) + tok, BF),
            struct((2,) + tok, BF),
        ],
        in_specs=[VM] * len(ins),
        out_specs=[VM] * 6,
        scratch_shapes=[
            pltpu.VMEM(smalls[0].shape, F32),
            pltpu.VMEM((job.half, wa), F32),
            pltpu.VMEM((rows, wa), F32),
            pltpu.VMEM((nt, rows, 2 * hd // nt), BF),
            pltpu.VMEM((nt - 1, rows, 2 * hd // nt), BF),
            pltpu.VMEM(smalls[0].shape, F32),
            pltpu.VMEM((total - 1,) + smalls[0].shape, F32),
            dma((5,)), dma((5,)), dma((3,)), dma((nt - 1,)), dma((nt - 1,)),
            dma((total - 1,)), dma((total - 1,)), dma((total - 1,)), dma((total - 1,)),
        ]
        + job.scratch(),
        compiler_params=pltpu.CompilerParams(
            collective_id=2, has_side_effects=True, vmem_limit_bytes=VMEM_LIMIT
        ),
    )(*ins)


def reduce_plain(grads_a, grads_m, smalls, ys, xs, nt, nd, hd):
    sec = lax.axis_index("section")
    pairs = [(0, 1), (1, 0)]

    def own_sum(pair):
        own = jnp.where(sec == 0, pair[0], pair[1])
        other = jnp.where(sec == 0, pair[1], pair[0])
        return own.astype(F32) + lax.ppermute(other, "section", pairs).astype(F32)

    def placed(pair):
        own = jnp.where(sec == 0, pair[0], pair[1])
        other = lax.ppermute(jnp.where(sec == 0, pair[1], pair[0]), "section", pairs)
        return jnp.stack([jnp.where(sec == 0, own, other), jnp.where(sec == 0, other, own)])

    g_a, g_m, small = own_sum(grads_a), own_sum(grads_m), own_sum(smalls)
    split = jnp.concatenate([g_a[:, : 2 * hd], g_m], axis=1).astype(BF)
    split = lax.psum_scatter(split, "dp", scatter_dimension=0, tiled=True).astype(F32)
    kv, small = lax.psum((g_a[:, 2 * hd :], small), ("tensor", "dp"))
    return split[:, : 2 * hd], split[:, 2 * hd :], kv, small, placed(ys), placed(xs)


def per_device(tokens, segments, cotangent, *weights):
    nt, nd = lax.axis_size("tensor"), lax.axis_size("dp")
    sec = lax.axis_index("section")
    width = tokens.shape[1]
    hd = weights[1].shape[-1]
    units = weights[4].shape[-1]
    rows = MB_TOK
    x16 = lax.dynamic_slice_in_dim(tokens, sec * rows, rows, 0)
    cot = lax.dynamic_slice_in_dim(cotangent, sec * rows, rows, 0)
    seg = lax.dynamic_slice_in_dim(segments, sec * rows, rows, 0)
    w0, w1 = both_layers(weights)
    at = jnp.arange(rows, dtype=jnp.int32)
    seen = (seg[:, None] == seg[None, :]) & (at[None, :] <= at[:, None])
    position = (jnp.sum(seen.astype(jnp.int32), axis=1) - 1).astype(F32)
    freq = jnp.exp(jnp.arange(hd // 2, dtype=F32) * (-2.0 * math.log(10000.0) / hd))
    angles = position[:, None] * freq[None, :]
    tables = (jnp.cos(angles), jnp.sin(angles), seg[:, None], seg[None, :])

    n2_0, *kept_0, att_0, res_0 = attend_forward(x16, w0, tables, nt, 3)
    y_0, gate_0, up_0, h_0, mlp_0 = feed_forward(n2_0, res_0, w0, None, nt, 4)
    n2_1, *kept_1, att_1, res_1 = attend_forward(y_0, w1, tables, nt, 3)
    y_1, d_mlp_1, gate_1, up_1, h_1, _, dg3_1 = feed_forward(n2_1, res_1, w1, cot, nt, 5)

    d_att_1, gm_1, dr_1, dg1_1, dg2_1, _, _ = feed_backward(
        d_mlp_1, cot, (n2_1, gate_1, up_1, h_1, res_1, att_1), w1, nt, 6
    )
    fits = width % (32 * nd) == 0 and (2 * hd // nt) % 128 == 0 and nt * nd <= 32
    dx_1, d_mlp_0, ga_1, dg0_1, dgq_1, dgk_1, _, _, _, dg3_0, *sum_m1 = attend_backward(
        d_att_1, dr_1, y_0, kept_1, w1, tables, (mlp_0, w0[7]), nt, 7, gm_1 if fits else None
    )
    d_att_0, gm_0, dr_0, dg1_0, dg2_0, _, _, *sum_a1 = feed_backward(
        d_mlp_0, dx_1, (n2_0, gate_0, up_0, h_0, res_0, att_0), w0, nt, 9, ga_1 if fits else None
    )
    dx_0, ga_0, dg0_0, dgq_0, dgk_0, _, _, _, *sum_m0 = attend_backward(
        d_att_0, dr_0, x16, kept_0, w0, tables, None, nt, 8, gm_0 if fits else None
    )
    if fits:
        ga_1, gm_0, gm_1 = sum_a1[0], sum_m0[0], sum_m1[0]

    def small(g0, g1, g2, g3, q, k):
        tail = ((0, 2), (0, width - hd))
        return jnp.concatenate([g0, g1, g2, g3, jnp.pad(jnp.concatenate([q, k]), tail)])

    smalls = (
        small(dg0_0, dg1_0, dg2_0, dg3_0, dgq_0, dgk_0),
        small(dg0_1, dg1_1, dg2_1, dg3_1, dgq_1, dgk_1),
    )
    reducer = reduce_all if fits else reduce_plain
    g_a, g_m, kv, sums, out_y, out_x = reducer(
        (ga_0, ga_1), (gm_0, gm_1), smalls, (y_0, y_1), (dx_0, dx_1), nt, nd, hd
    )
    if fits:
        kv = kv.reshape(nd, nt, width // nd, 2 * hd // nt).transpose(0, 2, 1, 3).reshape(width, 2 * hd)
        kv = kv.astype(F32)
    cols = width // nd
    gains = lax.dynamic_slice(sums, (0, lax.axis_index("dp") * cols), (4, cols))
    return (
        out_y.astype(F32).reshape(1, 2 * rows, width),
        out_x.astype(F32).reshape(1, 2 * rows, width),
        g_a[None, :, :hd],
        kv[None, :, :hd],
        kv[None, :, hd:],
        g_a[:, hd:].T[None],
        g_m[None, :, :units],
        g_m[None, :, units : 2 * units],
        g_m[:, 2 * units :].T[None],
        gains[None],
        sums[None, 4:6, :hd],
    )


def solution(mesh):
    return jax.shard_map(
        per_device,
        mesh=mesh,
        in_specs=(
            P("dp", None),
            P("dp"),
            P("dp", None),
            P("section", None, "tensor"),
            P("section", None, None),
            P("section", None, None),
            P("section", "tensor", None),
            P("section", None, "tensor"),
            P("section", None, "tensor"),
            P("section", "tensor", None),
            P("section", None, None),
            P("section", None, None),
        ),
        out_specs=(
            P("section", "dp", None),
            P("section", "dp", None),
            P("section", "dp", "tensor"),
            P("section", None, None),
            P("section", None, None),
            P("section", "tensor", "dp"),
            P("section", "dp", "tensor"),
            P("section", "dp", "tensor"),
            P("section", "tensor", "dp"),
            P("section", None, "dp"),
            P("section", None, None),
        ),
        check_vma=False,
    )
```
